128 devices in a mesh: ctx: 32 (over y, z, core), head: 4 (over x).
Axes of the slice: x: 4, y: 4, z: 4, core: 2. Of those that a mesh axis runs over, the one named last changes fastest.
Arguments:
- dout: bfloat16 [8192, 4096], P('ctx', 'head')
- out_weight: bfloat16 [4096, 8192], P('ctx', 'head'), may hold values from -0.0625 to 0.0625
- x_in: bfloat16 [8192, 8192], P('ctx', 'head'), may hold values from -6 to 6
- z_in: bfloat16 [8192, 8192], P('ctx', 'head'), may hold values from -6 to 6
- b_in: bfloat16 [8192, 1024], P('ctx', 'head'), may hold values from -6 to 6
- c_in: bfloat16 [8192, 1024], P('ctx', 'head'), may hold values from -6 to 6
- dt: float32 [8192, 128], P('ctx', 'head'), may hold values from 0 to 0.75, as said below
- rate: float32 [128], P('head'), may hold values from 0.5 to 2, as said below
- skip: float32 [128], P('head'), may hold values from 0.5 to 1.5
- gain: float32 [8192], P('head'), may hold values from 0.5 to 1.5
- start_state: float32 [32, 128, 64, 128], P('ctx', 'head'), may hold values from -3 to 3
Outputs:
- grad_x: bfloat16 [8192, 8192], P('ctx', 'head')
- grad_z: bfloat16 [8192, 8192], P('ctx', 'head')
- grad_b: bfloat16 [8192, 1024], P('ctx', 'head')
- grad_c: bfloat16 [8192, 1024], P('ctx', 'head')
- grad_dt: float32 [8192, 128], P('ctx', 'head')
- grad_w: bfloat16 [4096, 8192], P('ctx', 'head')
- grad_gain: float32 [8192], P('head')
- grad_rate: float32 [128], P('head')
- grad_skip: float32 [128], P('head')
- grad_start: float32 [32, 128, 64, 128], P('ctx', 'head')
The draws below stay inside these ranges and needn't reach their ends.
Inputs may be any that keep to these rules, and one draw needn't show every extreme that they name: `rate`: positive decay rates of each head. `dt`: positive step sizes.
All inputs are finite; a program needn't handle non-finite values.
Results may differ from the reference program's by a relative error of at most 0.025.
Values may be sent and summed in bfloat16 or wider, within the bound.
No kernel may reach another device: no remote copies, remote signals or barrier semaphores. Data moves between devices by JAX's collectives and lax.ppermute only.
A program may use at most 192 MiB of HBM per device.

```python
import math
import jax
import jax.numpy as jnp
from jax import lax

DM = 4096
MIXER_HEADS = 128
P_SIZE = 64
N = 128
G = 8
Q = 128
TOK_DEV = 256
DI = 8192
SEQUENCE_TOKENS = 8192
N_CTX = 32


def decay_profile(key, fast_share):
    key = jax.random.fold_in(key, 11)
    pick, level, spread = jax.random.split(key, 3)
    rate_values = jnp.exp(jax.random.uniform(spread, (MIXER_HEADS,), jnp.float32, math.log(0.5), math.log(2.0)))
    fast = jax.random.uniform(pick, (MIXER_HEADS,), jnp.float32) < fast_share
    fraction = jax.random.uniform(level, (MIXER_HEADS,), jnp.float32)
    quick = 1.0 / (50.0 - 20.0 * fraction)
    slow = (0.2 + 0.6 * fraction) / SEQUENCE_TOKENS
    return (rate_values, jnp.where(fast, quick, slow) / rate_values)


def draw_rate(key, part):
    share = 0.5
    rate_values, level_values = decay_profile(key, share)
    return rate_values


def draw_dt(key, part):
    share = 0.5
    rate_values, level_values = decay_profile(key, share)
    key = jax.random.fold_in(key, 23)
    jagged_profile, block_shaped, location_random_key, spike_random_key = jax.random.split(key, 4)
    segments = SEQUENCE_TOKENS // TOK_DEV
    token_multiplier = jnp.exp(jax.random.uniform(jagged_profile, (SEQUENCE_TOKENS, MIXER_HEADS), jnp.float32, math.log(0.5), math.log(2.0)))
    block_multiplier = jnp.exp(jax.random.uniform(block_shaped, (segments, MIXER_HEADS), jnp.float32, math.log(0.5), math.log(2.0)))
    block_multiplier = jnp.repeat(block_multiplier, TOK_DEV, axis=0)
    places = jax.random.randint(location_random_key, (3,), 0, SEQUENCE_TOKENS)
    spike_hits = jnp.any(jnp.arange(SEQUENCE_TOKENS)[:, None] == places[None, :], axis=1)
    spike_events = jax.random.uniform(spike_random_key, (SEQUENCE_TOKENS, MIXER_HEADS), jnp.float32, 0.22, 0.36) / rate_values
    return jnp.where(spike_hits[:, None], spike_events, level_values * token_multiplier * block_multiplier)


def draw_dout(key, part):
    key = jax.random.fold_in(key, 37)
    noise_key = jax.random.fold_in(key, 0)
    segments = SEQUENCE_TOKENS // TOK_DEV
    position = (jnp.arange(SEQUENCE_TOKENS) // TOK_DEV).astype(jnp.float32) / max(segments - 1, 1)
    ramp = 0.6 * 3.0 ** position
    noise = jax.random.normal(noise_key, (SEQUENCE_TOKENS, DM), jnp.float32)
    return (noise * ramp[:, None]).astype(jnp.bfloat16)


def steps_of(key, shape, shards, low, top_value):
    level, own = 1.0, jax.random.fold_in(key, 6)
    for axis_at, parts in shards:
        heights = jnp.exp(jax.random.uniform(jax.random.fold_in(own, axis_at), (parts,), jnp.float32, low / len(shards), top_value / len(shards)))
        level = level * jnp.repeat(heights, shape[axis_at] // parts).reshape([-1 if axis == axis_at else 1 for axis in range(len(shape))])
    return level


def gaussian(stream_key, dims, scale, limit, shards=(), kind=jnp.bfloat16):
    values = scale * jax.random.normal(stream_key, dims, jnp.float32)
    if shards:
        values = values * steps_of(stream_key, dims, shards, -0.22, 0.18)
    return jnp.clip(values, -limit, limit).astype(kind)


def setup_inputs(seed: int = 0) -> dict:
    splits = jax.random.split(jax.random.key(seed), 12)
    return {
        "dout": draw_dout(jax.random.fold_in(splits[11], 71), 0),
        "out_weight": gaussian(splits[1], (DM, DI), DI ** -0.5, 0.0625, ((0, 32), (1, 4))),
        "x_in": gaussian(splits[2], (SEQUENCE_TOKENS, DI), 1.0, 6.0, ((0, 32), (1, 4))),
        "z_in": gaussian(splits[3], (SEQUENCE_TOKENS, DI), 1.0, 6.0, ((0, 32), (1, 4))),
        "b_in": gaussian(splits[4], (SEQUENCE_TOKENS, G * N), 1.0, 6.0, ((0, 32), (1, 4))),
        "c_in": gaussian(splits[5], (SEQUENCE_TOKENS, G * N), 1.0, 6.0, ((0, 32), (1, 4))),
        "dt": draw_dt(jax.random.fold_in(splits[11], 71), 0),
        "rate": draw_rate(jax.random.fold_in(splits[11], 71), 0),
        "skip": jnp.clip(0.5 + 1.0 * jax.random.uniform(splits[8], (MIXER_HEADS,), jnp.float32) ** steps_of(splits[8], (MIXER_HEADS,), ((0, 4),), -0.2, 0.2), 0.5, 1.5),
        "gain": jnp.clip(1.0 + 0.1 * jax.random.normal(splits[9], (DI,), jnp.float32), 0.5, 1.5),
        "start_state": gaussian(splits[10], (N_CTX, MIXER_HEADS, P_SIZE, N), 0.3, 3.0, ((0, 32), (1, 4)), jnp.float32),
    }


highest = lax.Precision.HIGHEST
epsilon = 1e-05

def segment_scan(values, steps, keys_in, reads, rate_values, skips, start):
    length, heads, width = values.shape
    groups, state = (keys_in.shape[1], keys_in.shape[2])
    per_group = heads // groups
    blocks = length // Q
    vals = values.reshape(blocks, Q, groups, per_group, width)
    step_sizes = steps.reshape(blocks, Q, groups, per_group)
    keys = keys_in.reshape(blocks, Q, groups, state)
    queries = reads.reshape(blocks, Q, groups, state)
    logs = -step_sizes * rate_values.reshape(groups, per_group)
    running = jnp.cumsum(logs, axis=1)
    lower = jnp.arange(Q)[:, None] >= jnp.arange(Q)[None, :]
    lower = lower[None, :, :, None, None]
    spread = running[:, :, None] - running[:, None, :]
    decays = jnp.where(lower, jnp.exp(jnp.where(lower, spread, 0.0)), 0.0)
    scores = jnp.einsum('cign,cjgn->cijg', queries, keys, precision=highest)
    mixing = decays * scores[..., None] * step_sizes[:, None]
    inner = jnp.einsum('cijgk,cjgkp->cigkp', mixing, vals, precision=highest)
    tails = jnp.exp(running[:, -1:] - running) * step_sizes
    block_states = jnp.einsum('cjgk,cjgkp,cjgn->cgkpn', tails, vals, keys, precision=highest)
    carried = start.reshape(groups, per_group, width, state)
    entering = []
    for block in range(blocks):
        entering.append(carried)
        carried = jnp.exp(running[block, -1])[..., None, None] * carried + block_states[block]
    entering = jnp.stack(entering)
    outer = jnp.einsum('cign,cgkpn->cigkp', queries, entering, precision=highest) * jnp.exp(running)[..., None]
    output = (inner + outer).reshape(length, heads, width) + skips[None, :, None] * values
    return (output, carried.reshape(heads, width, state))

def gated_norm(output, gates, gains, groups):
    length = output.shape[0]
    gated = output.reshape(length, -1) * jax.nn.silu(gates)
    grouped = gated.reshape(length, groups, -1)
    power = lax.optimization_barrier(jnp.mean(grouped * grouped, axis=-1, keepdims=True))
    return (grouped * lax.rsqrt(power + epsilon)).reshape(length, -1) * gains

def window(array, lead, first, count, width):
    return lax.dynamic_slice(array, (lead, first), (count, width))

def reference(dout, out_weight, x_in, z_in, b_in, c_in, dt, rate, skip, gain, start_state):
    segments = start_state.shape[0]
    channels = DI // G
    per_group = MIXER_HEADS // G

    def one_group(group):
        first = (group * channels).astype(jnp.int32)
        head_first = (group * per_group).astype(jnp.int32)
        state_first = (group * N).astype(jnp.int32)
        zero_index = jnp.zeros((), jnp.int32)
        weights = lax.dynamic_slice_in_dim(out_weight, first, channels, 1)
        rate_values = lax.dynamic_slice_in_dim(rate, head_first, per_group, 0)
        skips = lax.dynamic_slice_in_dim(skip, head_first, per_group, 0)
        gains = lax.dynamic_slice_in_dim(gain, first, channels, 0)

        def local(values, gates, steps, keys_in, reads, rate_part, skip_part, gain_part, start):
            output, final = segment_scan(values.reshape(TOK_DEV, per_group, P_SIZE), steps, keys_in[:, None], reads[:, None], rate_part, skip_part, start)
            return (gated_norm(output, gates, gain_part, 1), final)

        def seg_step(carry, segment):
            end_grad, weight_grad, gain_grad, rate_grad, skip_grad = carry
            lead = (segment * TOK_DEV).astype(jnp.int32)
            douts = lax.dynamic_slice_in_dim(dout, lead, TOK_DEV, 0)
            upstream = jnp.dot(douts, weights, preferred_element_type=jnp.float32)
            values = window(x_in, lead, first, TOK_DEV, channels).astype(jnp.float32)
            gates = window(z_in, lead, first, TOK_DEV, channels).astype(jnp.float32)
            steps = window(dt, lead, head_first, TOK_DEV, per_group)
            keys_in = window(b_in, lead, state_first, TOK_DEV, N).astype(jnp.float32)
            reads = window(c_in, lead, state_first, TOK_DEV, N).astype(jnp.float32)
            start = lax.dynamic_slice(start_state, (segment.astype(jnp.int32), head_first, zero_index, zero_index), (1, per_group, P_SIZE, N))[0]
            (normed, final), back = jax.vjp(local, values, gates, steps, keys_in, reads, rate_values, skips, gains, start)
            grads = back((upstream, end_grad))
            term = jnp.dot(douts.T, normed.astype(jnp.bfloat16), preferred_element_type=jnp.float32)
            term = lax.optimization_barrier(term.astype(jnp.bfloat16)).astype(jnp.float32)
            carry = (grads[8], weight_grad + term, gain_grad + grads[7], rate_grad + grads[5], skip_grad + grads[6])
            results = (grads[0].astype(jnp.bfloat16), grads[1].astype(jnp.bfloat16), grads[3].astype(jnp.bfloat16), grads[4].astype(jnp.bfloat16), grads[2], grads[8])
            return (carry, results)
        initial = (jnp.zeros((per_group, P_SIZE, N), jnp.float32), jnp.zeros((DM, channels), jnp.float32), jnp.zeros((channels,), jnp.float32), jnp.zeros((per_group,), jnp.float32), jnp.zeros((per_group,), jnp.float32))
        order = jnp.arange(segments - 1, -1, -1, dtype=jnp.int32)
        final_carry, results = lax.scan(seg_step, initial, order)
        results = jax.tree.map(lambda leaf: jnp.flip(leaf, 0), results)
        grad_x = results[0].reshape(SEQUENCE_TOKENS, channels)
        grad_z = results[1].reshape(SEQUENCE_TOKENS, channels)
        grad_b = results[2].reshape(SEQUENCE_TOKENS, N)
        grad_c = results[3].reshape(SEQUENCE_TOKENS, N)
        grad_dt = results[4].reshape(SEQUENCE_TOKENS, per_group)
        return (grad_x, grad_z, grad_b, grad_c, grad_dt, final_carry[1].astype(jnp.bfloat16), final_carry[2], final_carry[3], final_carry[4], results[5])
    stacked = lax.map(one_group, jnp.arange(G, dtype=jnp.int32))
    grad_x = stacked[0].transpose(1, 0, 2).reshape(SEQUENCE_TOKENS, DI)
    grad_z = stacked[1].transpose(1, 0, 2).reshape(SEQUENCE_TOKENS, DI)
    grad_b = stacked[2].transpose(1, 0, 2).reshape(SEQUENCE_TOKENS, G * N)
    grad_c = stacked[3].transpose(1, 0, 2).reshape(SEQUENCE_TOKENS, G * N)
    grad_dt = stacked[4].transpose(1, 0, 2).reshape(SEQUENCE_TOKENS, MIXER_HEADS)
    grad_w = stacked[5].transpose(1, 0, 2).reshape(DM, DI)
    grad_gain = stacked[6].reshape(DI)
    grad_rate = stacked[7].reshape(MIXER_HEADS)
    grad_skip = stacked[8].reshape(MIXER_HEADS)
    grad_start = stacked[9].transpose(1, 0, 2, 3, 4).reshape(segments, MIXER_HEADS, P_SIZE, N)
    return (grad_x, grad_z, grad_b, grad_c, grad_dt, grad_w, grad_gain, grad_rate, grad_skip, grad_start)
```

```python
import jax
import jax.numpy as jnp
from jax import lax
from jax.experimental import pallas as pl
from jax.experimental.pallas import tpu as pltpu
from jax.sharding import PartitionSpec as P

P_SIZE = 64
N = 128
Q = 128
TOKENS = 256
HEADS = 32
GROUPS = 2
PER_GROUP = HEADS // GROUPS
CHANNELS = HEADS * P_SIZE
GROUP_CHANNELS = PER_GROUP * P_SIZE
PAIRS = HEADS // 2
GROUP_PAIRS = PER_GROUP // 2
STATE_ROWS = PER_GROUP * P_SIZE
EPSILON = 1e-05

f32 = jnp.float32
bf16 = jnp.bfloat16


def dot(a, b, over=((1,), (0,))):
    return lax.dot_general(a, b, (over, ((), ())), preferred_element_type=f32)


def dot_rows(a, b):
    return dot(a, b, ((1,), (1,)))


def dot_columns(a, b):
    return dot(a, b, ((0,), (0,)))


def iota(shape, axis):
    return lax.broadcasted_iota(jnp.int32, shape, axis)


def split2(v):
    high = v.astype(bf16)
    return high, (v - high.astype(f32)).astype(bf16)


def split3(v):
    high = v.astype(bf16)
    rest = v - high.astype(f32)
    middle = rest.astype(bf16)
    return high, middle, (rest - middle.astype(f32)).astype(bf16)


def exact_rows(rows, right):
    product = dot(jnp.concatenate(split3(rows), axis=0), right)
    return product[:HEADS] + product[HEADS : 2 * HEADS] + product[2 * HEADS :]


def part_columns(rows):
    parts = [part.astype(f32) for part in split3(rows)]
    stacked = jnp.concatenate(parts + [jnp.zeros_like(rows)], axis=0)
    return stacked.T.astype(bf16)


def pair_select(pair, width):
    row = iota((128, 2 * width), 0)
    head = 2 * pair + jnp.where(iota((128, 2 * width), 1) >= width, 1, 0)
    hit = ((row & (HEADS - 1)) == head) & (row < 3 * HEADS)
    return jnp.where(hit, 1.0, 0.0).astype(bf16)


def pair_sums(values, pair):
    row, lane = iota((128, 128), 0), iota((128, 128), 1)
    head = 2 * pair + jnp.where(row >= P_SIZE, 1, 0)
    place = jnp.where(lane == head, 1.0, 0.0).astype(bf16)
    high, low = split2(values)
    return dot(jnp.concatenate([high, low], axis=1), jnp.concatenate([place, place], axis=0))


def lanes_of(pair):
    return pl.ds(pl.multiple_of(pair * 128, 128), 128)


def halves(v):
    first = iota(v.shape, 1) < P_SIZE
    zero = jnp.zeros_like(v)
    return jnp.where(first, v, zero), jnp.where(first, zero, v)


def causal_exp(spread, keep):
    return jnp.exp(jnp.where(keep, spread, -1e30))


def forward_kernel(
    x_ref, z_ref, b_ref, c_ref, dt_ref, rate_ref, state_ref, gain_ref, skip_ref,
    y_ref, normed_ref, run_ref, run_col_ref, dt_col_ref,
    scores, gated_ref, power,
):
    steps = dt_ref[...]
    upto = jnp.where(iota((TOKENS, TOKENS), 0) <= iota((TOKENS, TOKENS), 1), 1.0, 0.0).astype(bf16)
    run = exact_rows(-steps * rate_ref[...], upto)
    run_ref[...] = run
    run_col_ref[...] = part_columns(run)
    dt_col_ref[...] = part_columns(steps)
    lower = iota((Q, Q), 0) >= iota((Q, Q), 1)
    for group in range(GROUPS):
        reads = c_ref[:, group * N : (group + 1) * N]
        scores[...] = dot_rows(reads, b_ref[:, group * N : (group + 1) * N])
        power[...] = jnp.zeros_like(power)

        def body(at, carry):
            pair = group * GROUP_PAIRS + at
            lanes = lanes_of(pair)
            own = pl.ds(pl.multiple_of(at * 128, 128), 128)
            xs = x_ref[:, lanes]
            expanded = dot(run_col_ref[...], pair_select(pair, 128))
            top, bottom = [], []
            for k in range(2):
                run_row = run_ref[pl.ds(2 * pair + k, 1), :]
                dt_row = dt_ref[pl.ds(2 * pair + k, 1), :]
                col = expanded[:, k * 128 : (k + 1) * 128]
                m00 = causal_exp(col[:Q] - run_row[:, :Q], lower) * (scores[:Q, :Q] * dt_row[:, :Q])
                m10 = jnp.exp(col[Q:] - run_row[:, :Q]) * (scores[Q:, :Q] * dt_row[:, :Q])
                m11 = causal_exp(col[Q:] - run_row[:, Q:], lower) * (scores[Q:, Q:] * dt_row[:, Q:])
                top.append(m00.astype(bf16))
                bottom.extend([m10.astype(bf16), m11.astype(bf16)])
            x0, x1 = halves(xs)
            y0 = dot(jnp.concatenate(top, axis=1), jnp.concatenate([x0[:Q], x1[:Q]], axis=0))
            y1 = dot(jnp.concatenate(bottom, axis=1), jnp.concatenate([x0, x1], axis=0))
            from_start = dot_rows(reads, state_ref[lanes, :].astype(bf16))
            first = iota((TOKENS, 128), 1) < P_SIZE
            reach = jnp.exp(jnp.where(first, expanded[:, :128], expanded[:, 128:]))
            y = jnp.concatenate([y0, y1], axis=0) + reach * from_start
            y = y + skip_ref[:, lanes] * xs.astype(f32)
            y_ref[:, lanes] = y
            gate = z_ref[:, lanes].astype(f32)
            gated = y * gate / (1.0 + jnp.exp(-gate))
            gated_ref[:, own] = gated
            power[...] += gated * gated
            return carry

        lax.fori_loop(0, GROUP_PAIRS, body, 0)
        mean = jnp.sum(power[...], axis=1, keepdims=True) * (1.0 / GROUP_CHANNELS)
        scale = jnp.broadcast_to(lax.rsqrt(mean + EPSILON), (TOKENS, 128))

        def finish(at, carry):
            lanes = lanes_of(group * GROUP_PAIRS + at)
            own = pl.ds(pl.multiple_of(at * 128, 128), 128)
            normed_ref[:, lanes] = (gated_ref[:, own] * scale * gain_ref[:, lanes]).astype(bf16)
            return carry

        lax.fori_loop(0, GROUP_PAIRS, finish, 0)


def norm_back_kernel(
    place_ref, own_ref, other_ref, y_ref, z_ref, c_ref, gain_ref, run_ref, run_col_ref,
    grad_y_ref, grad_z_ref, gain_sum_ref, start_ref, keep_ref, send_ref,
    power, along, decay,
):
    total = jnp.exp(run_ref[:, TOKENS - 1 : TOKENS])
    decay[...] = jnp.broadcast_to(total, (HEADS, 128))
    for group in range(GROUPS):
        reads = c_ref[:, group * N : (group + 1) * N]
        power[...] = jnp.zeros_like(power)
        along[...] = jnp.zeros_like(along)

        def pieces(at):
            pair = group * GROUP_PAIRS + at
            lanes = lanes_of(pair)
            upstream = own_ref[:, lanes] + other_ref[:, lanes].astype(f32)
            gate = z_ref[:, lanes].astype(f32)
            sigmoid = 1.0 / (1.0 + jnp.exp(-gate))
            y = y_ref[:, lanes]
            return pair, lanes, upstream, gate, sigmoid, y, y * gate * sigmoid

        def first(at, carry):
            pair, lanes, upstream, gate, sigmoid, y, gated = pieces(at)
            power[...] += gated * gated
            along[...] += upstream * gain_ref[:, lanes] * gated
            return carry

        lax.fori_loop(0, GROUP_PAIRS, first, 0)
        mean = jnp.sum(power[...], axis=1, keepdims=True) * (1.0 / GROUP_CHANNELS)
        scale = lax.rsqrt(mean + EPSILON)
        shared = jnp.sum(along[...], axis=1, keepdims=True) * (1.0 / GROUP_CHANNELS)
        pull = jnp.broadcast_to(scale * scale * scale * shared, (TOKENS, 128))
        scale = jnp.broadcast_to(scale, (TOKENS, 128))

        def second(at, carry):
            pair, lanes, upstream, gate, sigmoid, y, gated = pieces(at)
            grad_gated = scale * (upstream * gain_ref[:, lanes]) - gated * pull
            grad_y = grad_gated * (gate * sigmoid)
            grad_y_ref[:, lanes] = grad_y.astype(bf16)
            slope = sigmoid * (1.0 + gate * (1.0 - sigmoid))
            grad_z_ref[:, lanes] = (grad_gated * y * slope).astype(bf16)
            gain_sum_ref[:, lanes] = jnp.sum(upstream * gated * scale, axis=0, keepdims=True)
            reach = jnp.exp(dot(run_col_ref[...], pair_select(pair, P_SIZE)))
            start_ref[lanes, :] = dot_columns((grad_y * reach).astype(bf16), reads)
            return carry

        lax.fori_loop(0, GROUP_PAIRS, second, 0)
    core = place_ref[3]
    for ref, group in ((keep_ref, core), (send_ref, 1 - core)):
        rows = pl.ds(pl.multiple_of(group * STATE_ROWS, STATE_ROWS), STATE_ROWS)
        ref[:STATE_ROWS, :] = start_ref[rows, :].astype(bf16)
        high, low = split2(decay[pl.ds(pl.multiple_of(group * PER_GROUP, PER_GROUP), PER_GROUP), :])
        ref[STATE_ROWS : STATE_ROWS + PER_GROUP, :] = high
        ref[STATE_ROWS + PER_GROUP :, :] = low


def decay_of(message):
    first = message[STATE_ROWS : STATE_ROWS + PER_GROUP, :].astype(f32)
    return first + message[STATE_ROWS + PER_GROUP :, :].astype(f32)


def by_head(decay):
    return jnp.broadcast_to(decay[:, None, :], (PER_GROUP, P_SIZE, N)).reshape(STATE_ROWS, N)


def put_message(ref, state, decay):
    ref[:STATE_ROWS, :] = state.astype(bf16)
    high, low = split2(decay)
    ref[STATE_ROWS : STATE_ROWS + PER_GROUP, :] = high
    ref[STATE_ROWS + PER_GROUP :, :] = low


def state_of(message):
    return message[:STATE_ROWS, :].astype(f32)


def chip_kernel(place_ref, keep_ref, got_ref, chip_ref, last_ref):
    leads = place_ref[3] == 0
    keep, got = keep_ref[...], got_ref[...]
    early, late = jnp.where(leads, keep, got), jnp.where(leads, got, keep)
    decay = decay_of(early)
    put_message(
        chip_ref, state_of(early) + by_head(decay) * state_of(late), decay * decay_of(late)
    )
    last_ref[...] = late


def row_kernel(place_ref, own_ref, one_ref, two_ref, three_ref, row_ref, after_ref, reach_ref, held):
    for k, ref in enumerate((own_ref, one_ref, two_ref, three_ref)):
        held[k] = ref[...]
    z = place_ref[2]
    state = after = jnp.zeros((STATE_ROWS, N), f32)
    decay = reach = jnp.ones((PER_GROUP, N), f32)
    for at in (3, 2, 1, 0):
        message = held[(at - z) & 3]
        here = decay_of(message)
        state = state_of(message) + by_head(here) * state
        decay = here * decay
        later = at > z
        after = jnp.where(later, state, after)
        reach = jnp.where(later, decay, reach)
    put_message(row_ref, state, decay)
    after_ref[...] = after
    reach_ref[...] = reach


def end_kernel(place_ref, one_ref, two_ref, three_ref, after_ref, reach_ref, last_ref, mine_ref, send_ref):
    state = jnp.zeros((STATE_ROWS, N), f32)
    for ref in (three_ref, two_ref, one_ref):
        message = ref[...]
        state = state_of(message) + by_head(decay_of(message)) * state
    late = after_ref[...] + by_head(reach_ref[...]) * state
    message = last_ref[...]
    early = state_of(message) + by_head(decay_of(message)) * late
    leads = place_ref[3] == 0
    mine_ref[...] = jnp.where(leads, early, late).astype(bf16)
    send_ref[...] = jnp.where(leads, late, early).astype(bf16)


def scan_back_kernel(
    x_ref, b_ref, c_ref, dt_ref, run_ref, run_col_ref, dt_col_ref, state_ref, grad_y_ref,
    inner_ref, grad_c_ref, grad_b_ref, row_ref, col_ref, skip_sum_ref,
    scores, back, reads_back, skips,
):
    upper = iota((Q, Q), 0) <= iota((Q, Q), 1)
    skips[...] = jnp.zeros_like(skips)
    col_ref[...] = jnp.zeros_like(col_ref)
    lane = iota((Q, 128), 1)
    for group in range(GROUPS):
        keys = b_ref[:, group * N : (group + 1) * N]
        reads = c_ref[:, group * N : (group + 1) * N]
        scores[...] = dot_rows(keys, reads)
        back[...] = jnp.zeros_like(back)
        reads_back[...] = jnp.zeros_like(reads_back)

        def body(at, carry):
            pair = group * GROUP_PAIRS + at
            lanes = lanes_of(pair)
            xs = x_ref[:, lanes].astype(f32)
            grads = grad_y_ref[:, lanes]
            step = dot(dt_col_ref[...], pair_select(pair, P_SIZE))
            scaled = halves((step * xs).astype(bf16))
            split = halves(grads)
            expanded = dot(run_col_ref[...], pair_select(pair, 128))
            top, bottom = [], []
            for k in range(2):
                head = 2 * pair + k
                run_row = run_ref[pl.ds(head, 1), :]
                col = expanded[:, k * 128 : (k + 1) * 128]
                d0 = dot_rows(scaled[k][:Q], grads)
                d11 = dot_rows(scaled[k][Q:], grads[Q:])
                l00 = causal_exp(run_row[:, :Q] - col[:Q], upper)
                l01 = jnp.exp(run_row[:, Q:] - col[:Q])
                l11 = causal_exp(run_row[:, Q:] - col[Q:], upper)
                p00, p01, p11 = l00 * d0[:, :Q], l01 * d0[:, Q:], l11 * d11
                back[:Q, :Q] += p00
                back[:Q, Q:] += p01
                back[Q:, Q:] += p11
                s00, s01, s11 = scores[:Q, :Q], scores[:Q, Q:], scores[Q:, Q:]
                w00, w01, w11 = p00 * s00, p01 * s01, p11 * s11
                row_ref[0, pl.ds(head, 1), :] = jnp.sum(w00, axis=0, keepdims=True)
                row_ref[1, pl.ds(head, 1), :] = jnp.sum(w01 + w11, axis=0, keepdims=True)
                col_ref[:Q, :] -= jnp.where(lane == head, jnp.sum(w00 + w01, axis=1, keepdims=True), 0.0)
                col_ref[Q:, :] -= jnp.where(lane == head, jnp.sum(w11, axis=1, keepdims=True), 0.0)
                top.extend([(l00 * s00).astype(bf16), (l01 * s01).astype(bf16)])
                bottom.append((l11 * s11).astype(bf16))
            inner_ref[:Q, lanes] = dot(jnp.concatenate(top, axis=1), jnp.concatenate(split, axis=0))
            inner_ref[Q:, lanes] = dot(
                jnp.concatenate(bottom, axis=1),
                jnp.concatenate([split[0][Q:], split[1][Q:]], axis=0),
            )
            state = state_ref[lanes, :].astype(bf16)
            first = iota((TOKENS, 128), 1) < P_SIZE
            reach = jnp.exp(jnp.where(first, expanded[:, :128], expanded[:, 128:]))
            wide = grads.astype(f32)
            reached = reach * wide
            reads_back[...] += dot(reached.astype(bf16), state)
            col_ref[...] += pair_sums(reached * dot_rows(reads, state), pair)
            skips[...] += pair_sums(xs * wide, pair)
            return carry

        lax.fori_loop(0, GROUP_PAIRS, body, 0)
        inner = back[...].astype(bf16)
        grad_b_ref[:, group * N : (group + 1) * N] = dot(inner, reads)
        grad_c_ref[:, group * N : (group + 1) * N] = (
            dot_columns(inner, keys) + reads_back[...]
        ).astype(bf16)
    skip_sum_ref[...] = jnp.sum(skips[...], axis=0, keepdims=True)


def end_back_kernel(
    place_ref, x_ref, b_ref, dt_ref, rate_ref, skip_ref, run_ref, run_col_ref, dt_col_ref,
    state_ref, grad_y_ref, inner_ref, keys_back_ref, row_ref, col_ref, skip_sum_ref,
    mine_ref, got_ref, start_ref, gain_sum_ref,
    grad_x_ref, grad_b_ref, grad_dt_ref, grad_start_ref, sums_ref,
    ends, decay, directs, tails, products,
):
    core = place_ref[3]
    ends[pl.ds(pl.multiple_of(core * STATE_ROWS, STATE_ROWS), STATE_ROWS), :] = mine_ref[...]
    ends[pl.ds(pl.multiple_of((1 - core) * STATE_ROWS, STATE_ROWS), STATE_ROWS), :] = got_ref[...]
    run = run_ref[...]
    total = jnp.exp(run[:, TOKENS - 1 : TOKENS])
    decay[...] = jnp.broadcast_to(total, (HEADS, 128))
    directs[...] = jnp.zeros_like(directs)
    tails[...] = jnp.zeros_like(tails)
    for group in range(GROUPS):
        keys = b_ref[:, group * N : (group + 1) * N]

        def body(at, keys_back):
            pair = group * GROUP_PAIRS + at
            lanes = lanes_of(pair)
            end = ends[lanes, :]
            wide_end = end.astype(f32)
            xs = x_ref[:, lanes].astype(f32)
            step = dot(dt_col_ref[...], pair_select(pair, P_SIZE))
            running = dot(run_col_ref[...], pair_select(pair, P_SIZE))
            tail = jnp.exp(running[TOKENS - 1 :, :] - running)
            read = dot_rows(keys, end)
            tailed = tail * (step * xs)
            grad_scaled = inner_ref[:, lanes] + tail * read
            grad_x = step * grad_scaled + skip_ref[:, lanes] * grad_y_ref[:, lanes].astype(f32)
            grad_x_ref[:, lanes] = grad_x.astype(bf16)
            directs[...] += pair_sums(xs * grad_scaled, pair)
            tails[...] += pair_sums(tailed * read, pair)
            product = wide_end * state_ref[lanes, :]
            for k in range(2):
                head = 2 * pair + k
                half = slice(k * P_SIZE, (k + 1) * P_SIZE)
                products[pl.ds(head, 1), :] = jnp.sum(product[half], axis=0, keepdims=True)
                rows = pl.ds(pl.multiple_of(head * P_SIZE, P_SIZE), P_SIZE)
                grad_start_ref[rows, :] = start_ref[rows, :] + decay[pl.ds(head, 1), :] * wide_end[half]
            return keys_back + dot(tailed.astype(bf16), end)

        keys_back = lax.fori_loop(
            0, GROUP_PAIRS, body, keys_back_ref[:, group * N : (group + 1) * N]
        )
        grad_b_ref[:, group * N : (group + 1) * N] = keys_back.astype(bf16)
    tail_rows = tails[...].T[:HEADS]
    shared = jnp.sum(tail_rows, axis=1, keepdims=True)
    shared = shared + total * jnp.sum(products[...], axis=1, keepdims=True)
    here = jnp.concatenate([row_ref[0], row_ref[1]], axis=1)
    here = here + col_ref[...].T[:HEADS] - tail_rows
    since = jnp.where(iota((TOKENS, TOKENS), 0) >= iota((TOKENS, TOKENS), 1), 1.0, 0.0).astype(bf16)
    grad_log = exact_rows(here, since) + shared
    grad_dt = directs[...].T[:HEADS] - rate_ref[...] * grad_log
    spent = -dt_ref[...] * grad_log
    zero = jnp.zeros_like(spent)
    columns = jnp.concatenate([grad_dt, spent, zero, zero], axis=0).T
    grad_dt_ref[...] = columns[:, :HEADS]
    sums = jnp.sum(columns, axis=0, keepdims=True)
    sums_ref[:, :CHANNELS] = gain_sum_ref[...]
    sums_ref[:, CHANNELS:] = jnp.where(iota((1, 128), 1) < HEADS, skip_sum_ref[...], sums)


def call(kernel, outs, scratch, scalars, *arrays, flops=0, seconds=0):
    vmem = pl.BlockSpec(memory_space=pltpu.VMEM)
    specs = [pl.BlockSpec(memory_space=pltpu.SMEM)] * scalars + [vmem] * (len(arrays) - scalars)
    size = sum(a.size * a.dtype.itemsize for a in arrays)
    size += sum(s[0][0] * s[0][1] * jnp.dtype(s[1]).itemsize for s in outs)
    return pl.pallas_call(
        kernel,
        out_shape=[jax.ShapeDtypeStruct(shape, kind) for shape, kind in outs],
        in_specs=specs,
        out_specs=[vmem] * len(outs),
        scratch_shapes=[pltpu.VMEM(shape, kind) for shape, kind in scratch],
        compiler_params=pltpu.CompilerParams(vmem_limit_bytes=56 * 2**20),
        cost_estimate=pl.CostEstimate(flops=flops, bytes_accessed=size, transcendentals=0),
    )(*arrays)


def forward(x, z, b, c, steps, rate, state, gain, skip):
    return call(
        forward_kernel,
        [((TOKENS, CHANNELS), f32), ((TOKENS, CHANNELS), bf16), ((HEADS, TOKENS), f32),
         ((TOKENS, 128), bf16), ((TOKENS, 128), bf16)],
        [((TOKENS, TOKENS), f32), ((TOKENS, GROUP_CHANNELS), f32), ((TOKENS, 128), f32)],
        0, x, z, b, c, steps, rate, state, gain, skip, flops=10**10,
    )


MESSAGE = ((STATE_ROWS + 2 * PER_GROUP, N), bf16)


def norm_back(place, own, other, y, z, c, gain, run, run_col):
    return call(
        norm_back_kernel,
        [((TOKENS, CHANNELS), bf16), ((TOKENS, CHANNELS), bf16), ((1, CHANNELS), f32),
         ((CHANNELS, N), f32), MESSAGE, MESSAGE],
        [((TOKENS, 128), f32), ((TOKENS, 128), f32), ((HEADS, 128), f32)],
        1, place, own, other, y, z, c, gain, run, run_col, flops=6 * 10**9,
    )


def chip_state(place, keep, got):
    return call(chip_kernel, [MESSAGE, MESSAGE], [], 1, place, keep, got)


def row_state(place, own, one, two, three):
    return call(
        row_kernel, [MESSAGE, ((STATE_ROWS, N), f32), ((PER_GROUP, N), f32)],
        [((4, STATE_ROWS + 2 * PER_GROUP, N), bf16)], 1, place, own, one, two, three,
    )


def end_state(place, one, two, three, after, reach, last):
    return call(
        end_kernel, [((STATE_ROWS, N), bf16)] * 2, [], 1, place, one, two, three, after, reach, last
    )


def scan_back(x, b, c, steps, run, run_col, dt_col, state, grad_y):
    return call(
        scan_back_kernel,
        [((TOKENS, CHANNELS), f32), ((TOKENS, GROUPS * N), bf16), ((TOKENS, GROUPS * N), f32),
         ((2, HEADS, Q), f32), ((TOKENS, 128), f32), ((1, 128), f32)],
        [((TOKENS, TOKENS), f32), ((TOKENS, TOKENS), f32), ((TOKENS, N), f32), ((TOKENS, 128), f32)],
        0, x, b, c, steps, run, run_col, dt_col, state, grad_y, flops=15 * 10**9,
    )


def end_back(place, *arrays):
    return call(
        end_back_kernel,
        [((TOKENS, CHANNELS), bf16), ((TOKENS, GROUPS * N), bf16), ((TOKENS, HEADS), f32),
         ((CHANNELS, N), f32), ((1, CHANNELS + 128), f32)],
        [((CHANNELS, N), bf16), ((HEADS, 128), f32), ((TOKENS, 128), f32), ((TOKENS, 128), f32),
         ((HEADS, 128), f32)],
        1, place, *arrays, flops=5 * 10**9,
    )


def split_kernel(place_ref, dout_ref, keep_ref, send_ref):
    leads = place_ref[3] == 0
    for at in range(4):
        even = dout_ref[:, 256 * at : 256 * at + 128]
        odd = dout_ref[:, 256 * at + 128 : 256 * at + 256]
        own = slice(128 * at, 128 * at + 128)
        keep_ref[:, own] = jnp.where(leads, even, odd)
        send_ref[:, own] = jnp.where(leads, odd, even)


def split_dout(place, dout):
    return call(split_kernel, [((TOKENS, 512), bf16)] * 2, [], 1, place, dout)


def weight_grad_kernel(place_ref, *refs):
    pieces, (own_ref, other_ref, out_ref, turned) = refs[:8], refs[8:]

    @pl.when(pl.program_id(0) == 0)
    def _():
        for at in range(4):
            for core in range(2):
                turned[at, :, core * TOKENS : (core + 1) * TOKENS] = pieces[2 * at + core][...].T

    right = jnp.concatenate([own_ref[...], other_ref[...]], axis=0)
    for at in range(4):
        origin = (place_ref[0] - at) & 3
        rows = pl.ds(pl.multiple_of(origin * 512, 512), 512)
        out_ref[rows, :] = dot(turned[at], right).astype(bf16)


def weight_grad(place, pieces, own, other):
    tile = 512
    return pl.pallas_call(
        weight_grad_kernel,
        grid=(CHANNELS // tile,),
        out_shape=jax.ShapeDtypeStruct((2048, CHANNELS), bf16),
        in_specs=[pl.BlockSpec(memory_space=pltpu.SMEM)]
        + [pl.BlockSpec((TOKENS, 512), lambda i: (0, 0))] * 8
        + [pl.BlockSpec((TOKENS, tile), lambda i: (0, i))] * 2,
        out_specs=pl.BlockSpec((2048, tile), lambda i: (0, i)),
        scratch_shapes=[pltpu.VMEM((4, 512, 512), bf16)],
        compiler_params=pltpu.CompilerParams(vmem_limit_bytes=56 * 2**20),
        cost_estimate=pl.CostEstimate(flops=2**32, bytes_accessed=12 * 2**20, transcendentals=0),
    )(place, *pieces, own, other)


def upstream_kernel(place_ref, *refs):
    pieces, (weight_ref, own_ref, other_ref) = refs[:8], refs[8:]
    total = jnp.zeros((2 * TOKENS, weight_ref.shape[1]), f32)
    for at in range(4):
        origin = (place_ref[0] - at) & 3
        rows = pl.ds(pl.multiple_of(origin * 512, 512), 512)
        left = jnp.concatenate([pieces[2 * at][...], pieces[2 * at + 1][...]], axis=0)
        total = total + dot(left, weight_ref[rows, :])
    own_ref[...] = total[:TOKENS]
    other_ref[...] = total[TOKENS:].astype(bf16)


def upstream_parts(place, pieces, weights):
    tile = 512
    return pl.pallas_call(
        upstream_kernel,
        grid=(CHANNELS // tile,),
        out_shape=[
            jax.ShapeDtypeStruct((TOKENS, CHANNELS), f32),
            jax.ShapeDtypeStruct((TOKENS, CHANNELS), bf16),
        ],
        in_specs=[pl.BlockSpec(memory_space=pltpu.SMEM)]
        + [pl.BlockSpec((TOKENS, 512), lambda i: (0, 0))] * 8
        + [pl.BlockSpec((2048, tile), lambda i: (0, i))],
        out_specs=[pl.BlockSpec((TOKENS, tile), lambda i: (0, i))] * 2,
        compiler_params=pltpu.CompilerParams(vmem_limit_bytes=56 * 2**20),
        cost_estimate=pl.CostEstimate(flops=2**32, bytes_accessed=13 * 2**20, transcendentals=0),
    )(place, *pieces, weights)


def device(y, z, core):
    return (y * 4 + z) * 2 + core


PLACES = [(y, z, core) for y in range(4) for z in range(4) for core in range(2)]
SAME_CORE = [[device(y, z, core) for y in range(4) for z in range(4)] for core in range(2)]
SWAP = [(device(y, z, core), device(y, z, 1 - core)) for y, z, core in PLACES]


def along_z(by):
    return [(device(y, z, core), device(y, (z + by) % 4, core)) for y, z, core in PLACES]


def along_y(by):
    return [(device(y, z, core), device((y + by) % 4, z, core)) for y, z, core in PLACES]


def earlier_y(by):
    return [(device(y, z, core), device(y - by, z, core)) for y, z, core in PLACES if y >= by]


def move(array, pairs):
    return lax.ppermute(array, "ctx", pairs)


def along_x(array, by):
    return lax.ppermute(array, "head", [(x, (x + by) % 4) for x in range(4)])


def gather_pieces(own, other):
    before, after = (along_x(own, 1), along_x(other, 1)), (along_x(own, -1), along_x(other, -1))
    return own, other, *before, along_x(before[0], 1), along_x(after[1], -1), *after


def sum_ctx(array):
    array = array + move(array, SWAP)
    array = array + move(array, along_z(1)) + move(array, along_z(2)) + move(array, along_z(3))
    return array + move(array, along_y(1)) + move(array, along_y(2)) + move(array, along_y(3))


def per_device(dout, out_weight, x_in, z_in, b_in, c_in, dt, rate, skip, gain, start_state):
    at = lax.axis_index("ctx")
    place = jnp.stack([lax.axis_index("head"), at // 8, (at // 2) % 4, at % 2]).astype(jnp.int32)
    weights = lax.all_gather(out_weight, "ctx", axis=0, tiled=True, axis_index_groups=SAME_CORE)
    own_dout, send_dout = split_dout(place, dout)
    pieces = gather_pieces(own_dout, move(send_dout, SWAP))
    steps = dt.T
    rates = rate.reshape(HEADS, 1)
    skips = jnp.repeat(skip, P_SIZE).reshape(1, CHANNELS)
    gains = gain.reshape(1, CHANNELS)
    state = start_state.reshape(CHANNELS, N)
    y, normed, run, run_col, dt_col = forward(
        x_in, z_in, b_in, c_in, steps, rates, state, gains, skips
    )
    term = weight_grad(place, pieces, normed, move(normed, SWAP))
    grad_w = lax.psum_scatter(
        term, "ctx", scatter_dimension=0, tiled=True, axis_index_groups=SAME_CORE
    )
    own_part, other_part = upstream_parts(place, pieces, weights)
    grad_y, grad_z, gain_sum, start, keep, send = norm_back(
        place, own_part, move(other_part, SWAP), y, z_in, c_in, gains, run, run_col
    )
    chip, last = chip_state(place, keep, move(send, SWAP))
    row, after, reach = row_state(place, chip, *[move(chip, along_z(-k)) for k in (1, 2, 3)])
    mine, theirs = end_state(
        place, *[move(row, earlier_y(k)) for k in (1, 2, 3)], after, reach, last
    )
    got = move(theirs, SWAP)
    inner, grad_c, keys_back, row_sums, col_sums, skip_sum = scan_back(
        x_in, b_in, c_in, steps, run, run_col, dt_col, state, grad_y
    )
    grad_x, grad_b, grad_dt, grad_start, sums = end_back(
        place, x_in, b_in, steps, rates, skips, run, run_col, dt_col, state, grad_y, inner,
        keys_back, row_sums, col_sums, skip_sum, mine, got, start, gain_sum,
    )
    sums = sum_ctx(sums)[0]
    return (
        grad_x,
        grad_z,
        grad_b,
        grad_c,
        grad_dt,
        grad_w,
        sums[:CHANNELS],
        sums[CHANNELS + HEADS : CHANNELS + 2 * HEADS],
        sums[CHANNELS : CHANNELS + HEADS],
        grad_start.reshape(start_state.shape),
    )


def solution(mesh):
    full, whole = P("ctx", "head"), P("head")
    state = P("ctx", "head", None, None)
    return jax.shard_map(
        per_device,
        mesh=mesh,
        in_specs=(full,) * 7 + (whole,) * 3 + (state,),
        out_specs=(full,) * 6 + (whole,) * 3 + (state,),
        check_vma=False,
    )
```

```python
import functools
import math

import jax
import jax.numpy as jnp
from jax import lax
from jax.experimental import pallas as pl
from jax.experimental.pallas import tpu as pltpu
from jax.sharding import PartitionSpec as P

P_SIZE = 64
N = 128
Q = 128
TOKENS = 256
HEADS = 32
GROUPS = 2
PER_GROUP = HEADS // GROUPS
CHANNELS = HEADS * P_SIZE
GROUP_CHANNELS = PER_GROUP * P_SIZE
PAIRS = HEADS // 2
GROUP_PAIRS = PER_GROUP // 2
STATE_ROWS = PER_GROUP * P_SIZE
EPSILON = 1e-05
UNROLL = 2
SHORT, LONG = 100000000, 20000000000

f32 = jnp.float32
bf16 = jnp.bfloat16


def dot(a, b, over=((1,), (0,))):
    return lax.dot_general(a, b, (over, ((), ())), preferred_element_type=f32)


def dot_rows(a, b):
    return dot(a, b, ((1,), (1,)))


def dot_columns(a, b):
    return dot(a, b, ((0,), (0,)))


def iota(shape, axis):
    return lax.broadcasted_iota(jnp.int32, shape, axis)


def split2(v):
    high = v.astype(bf16)
    return high, (v - high.astype(f32)).astype(bf16)


def split3(v):
    high = v.astype(bf16)
    rest = v - high.astype(f32)
    middle = rest.astype(bf16)
    return high, middle, (rest - middle.astype(f32)).astype(bf16)


def exact_rows(rows, right):
    product = dot(jnp.concatenate(split3(rows), axis=0), right)
    return product[:HEADS] + product[HEADS : 2 * HEADS] + product[2 * HEADS :]


def part_columns(rows):
    parts = [part.astype(f32) for part in split3(rows)]
    stacked = jnp.concatenate(parts + [jnp.zeros_like(rows)], axis=0)
    return stacked.T.astype(bf16)


def pair_select(pair, width):
    row = iota((128, 2 * width), 0)
    head = 2 * pair + jnp.where(iota((128, 2 * width), 1) >= width, 1, 0)
    hit = ((row & (HEADS - 1)) == head) & (row < 3 * HEADS)
    return jnp.where(hit, 1.0, 0.0).astype(bf16)


def pair_sums(values, pair):
    row, lane = iota((128, 128), 0), iota((128, 128), 1)
    head = 2 * pair + jnp.where(row >= P_SIZE, 1, 0)
    place = jnp.where(lane == head, 1.0, 0.0).astype(bf16)
    high, low = split2(values)
    return dot(jnp.concatenate([high, low], axis=1), jnp.concatenate([place, place], axis=0))


def lanes_of(pair):
    return pl.ds(pl.multiple_of(pair * 128, 128), 128)


def halves(v):
    first = iota(v.shape, 1) < P_SIZE
    zero = jnp.zeros_like(v)
    return jnp.where(first, v, zero), jnp.where(first, zero, v)


def causal_exp(spread, keep):
    return jnp.exp(jnp.where(keep, spread, -1e30))


def prepare_kernel(place_ref, dout_ref, dt_ref, rate_ref, keep_ref, send_ref, run_ref, run_col_ref, dt_col_ref):
    leads = place_ref[3] == 0
    for at in range(4):
        even = dout_ref[:, 256 * at : 256 * at + 128]
        odd = dout_ref[:, 256 * at + 128 : 256 * at + 256]
        own = slice(128 * at, 128 * at + 128)
        keep_ref[:, own] = jnp.where(leads, even, odd)
        send_ref[:, own] = jnp.where(leads, odd, even)
    steps = dt_ref[...]
    upto = jnp.where(iota((TOKENS, TOKENS), 0) <= iota((TOKENS, TOKENS), 1), 1.0, 0.0).astype(bf16)
    run = exact_rows(-steps * rate_ref[...], upto)
    run_ref[...] = run
    run_col_ref[...] = part_columns(run)
    dt_col_ref[...] = part_columns(steps)


def forward_kernel(
    group, x_ref, z_ref, b_ref, c_ref, dt_ref, run_ref, run_col_ref, state_ref, gain_ref, skip_ref,
    y_ref, normed_ref,
    scores, gated_ref, power,
):
    lower = iota((Q, Q), 0) >= iota((Q, Q), 1)
    reads = c_ref[...]
    scores[...] = dot_rows(reads, b_ref[...])
    power[...] = jnp.zeros_like(power)

    def body(at, carry):
        pair = group * GROUP_PAIRS + at
        lanes = own = lanes_of(at)
        xs = x_ref[:, lanes]
        expanded = dot(run_col_ref[...], pair_select(pair, 128))
        top, bottom = [], []
        for k in range(2):
            run_row = run_ref[pl.ds(2 * pair + k, 1), :]
            dt_row = dt_ref[pl.ds(2 * pair + k, 1), :]
            col = expanded[:, k * 128 : (k + 1) * 128]
            m00 = causal_exp(col[:Q] - run_row[:, :Q], lower) * (scores[:Q, :Q] * dt_row[:, :Q])
            m10 = jnp.exp(col[Q:] - run_row[:, :Q]) * (scores[Q:, :Q] * dt_row[:, :Q])
            m11 = causal_exp(col[Q:] - run_row[:, Q:], lower) * (scores[Q:, Q:] * dt_row[:, Q:])
            top.append(m00.astype(bf16))
            bottom.extend([m10.astype(bf16), m11.astype(bf16)])
        x0, x1 = halves(xs)
        y0 = dot(jnp.concatenate(top, axis=1), jnp.concatenate([x0[:Q], x1[:Q]], axis=0))
        y1 = dot(jnp.concatenate(bottom, axis=1), jnp.concatenate([x0, x1], axis=0))
        from_start = dot_rows(reads, state_ref[lanes_of(pair), :].astype(bf16))
        first = iota((TOKENS, 128), 1) < P_SIZE
        reach = jnp.exp(jnp.where(first, expanded[:, :128], expanded[:, 128:]))
        y = jnp.concatenate([y0, y1], axis=0) + reach * from_start
        y = y + skip_ref[:, lanes] * xs.astype(f32)
        y_ref[:, lanes] = y
        gate = z_ref[:, lanes].astype(f32)
        gated = y * gate / (1.0 + jnp.exp(-gate))
        gated_ref[:, own] = gated
        power[...] += gated * gated
        return carry

    lax.fori_loop(0, GROUP_PAIRS, body, 0, unroll=UNROLL)
    mean = jnp.sum(power[...], axis=1, keepdims=True) * (1.0 / GROUP_CHANNELS)
    scale = jnp.broadcast_to(lax.rsqrt(mean + EPSILON), (TOKENS, 128))

    def finish(at, carry):
        lanes = own = lanes_of(at)
        normed_ref[:, lanes] = (gated_ref[:, own] * scale * gain_ref[:, lanes]).astype(bf16)
        return carry

    lax.fori_loop(0, GROUP_PAIRS, finish, 0, unroll=UNROLL)


def norm_back_kernel(
    group, place_ref, own_ref, other_ref, y_ref, z_ref, c_ref, gain_ref, run_ref, run_col_ref, *rest
):
    first_ref, rest = (rest[0], rest[1:]) if group else (None, rest)
    grad_y_ref, grad_z_ref, gain_sum_ref, start_ref = rest[:4]
    outs, (power, along) = rest[4:-2], rest[-2:]
    reads = c_ref[...]
    power[...] = jnp.zeros_like(power)
    along[...] = jnp.zeros_like(along)

    def pieces(at):
        lanes = lanes_of(at)
        upstream = own_ref[:, lanes] + other_ref[:, lanes].astype(f32)
        gate = z_ref[:, lanes].astype(f32)
        sigmoid = 1.0 / (1.0 + jnp.exp(-gate))
        y = y_ref[:, lanes]
        return lanes, upstream, gate, sigmoid, y, y * gate * sigmoid

    def first(at, carry):
        lanes, upstream, gate, sigmoid, y, gated = pieces(at)
        power[...] += gated * gated
        along[...] += upstream * gain_ref[:, lanes] * gated
        return carry

    lax.fori_loop(0, GROUP_PAIRS, first, 0, unroll=UNROLL)
    mean = jnp.sum(power[...], axis=1, keepdims=True) * (1.0 / GROUP_CHANNELS)
    scale = lax.rsqrt(mean + EPSILON)
    shared = jnp.sum(along[...], axis=1, keepdims=True) * (1.0 / GROUP_CHANNELS)
    pull = jnp.broadcast_to(scale * scale * scale * shared, (TOKENS, 128))
    scale = jnp.broadcast_to(scale, (TOKENS, 128))

    def second(at, carry):
        lanes, upstream, gate, sigmoid, y, gated = pieces(at)
        grad_gated = scale * (upstream * gain_ref[:, lanes]) - gated * pull
        grad_y = grad_gated * (gate * sigmoid)
        grad_y_ref[:, lanes] = grad_y.astype(bf16)
        slope = sigmoid * (1.0 + gate * (1.0 - sigmoid))
        grad_z_ref[:, lanes] = (grad_gated * y * slope).astype(bf16)
        gain_sum_ref[:, lanes] = jnp.sum(upstream * gated * scale, axis=0, keepdims=True)
        pair = group * GROUP_PAIRS + at
        reach = jnp.exp(dot(run_col_ref[...], pair_select(pair, P_SIZE)))
        start_ref[lanes, :] = dot_columns((grad_y * reach).astype(bf16), reads)
        return carry

    lax.fori_loop(0, GROUP_PAIRS, second, 0, unroll=UNROLL)
    total = jnp.exp(run_ref[group * PER_GROUP : (group + 1) * PER_GROUP, TOKENS - 1 :])
    high, low = split2(jnp.broadcast_to(total, (PER_GROUP, 128)))
    states = start_ref[...].astype(bf16)
    if first_ref is None:
        ref = outs[0]
        ref[:STATE_ROWS, :] = states
        ref[STATE_ROWS : STATE_ROWS + PER_GROUP, :] = high
        ref[STATE_ROWS + PER_GROUP :, :] = low
    else:
        message = jnp.concatenate([states, high, low], axis=0)
        leads = place_ref[3] == 0
        outs[0][...] = jnp.where(leads, first_ref[...], message)
        outs[1][...] = jnp.where(leads, message, first_ref[...])


QUARTER = STATE_ROWS // 4
QUARTER_HEADS = PER_GROUP // 4


def by_head(decay):
    heads = decay.shape[0]
    return jnp.broadcast_to(decay[:, None, :], (heads, P_SIZE, N)).reshape(heads * P_SIZE, N)


def decay_of(message):
    first = message[STATE_ROWS : STATE_ROWS + PER_GROUP, :].astype(f32)
    return first + message[STATE_ROWS + PER_GROUP :, :].astype(f32)


def state_of(message):
    return message[:STATE_ROWS, :].astype(f32)


def put_quarter(ref, state, decay):
    ref[:QUARTER, :] = state.astype(bf16)
    high, low = split2(decay)
    ref[QUARTER:, :] = jnp.concatenate([high.astype(f32), low.astype(f32)], axis=0).astype(bf16)


def quarter_of(message):
    decay = message[QUARTER:, :].astype(f32)
    return message[:QUARTER, :].astype(f32), decay[:8] + decay[8:]


def chip_kernel(place_ref, keep_ref, got_ref, *refs):
    outs, last_ref, states, decays = refs[:4], refs[4], refs[5], refs[6]
    leads = place_ref[3] == 0
    keep, got = keep_ref[...], got_ref[...]
    early, late = jnp.where(leads, keep, got), jnp.where(leads, got, keep)
    decay = decay_of(early)
    states[...] = state_of(early) + by_head(decay) * state_of(late)
    decay = decay * decay_of(late)
    decays[...] = jnp.zeros_like(decays)
    for at in range(4):
        decays[at, :QUARTER_HEADS, :] = decay[at * QUARTER_HEADS : (at + 1) * QUARTER_HEADS]
    for by, ref in enumerate(outs):
        at = (place_ref[2] + by) & 3
        put_quarter(ref, states[pl.ds(pl.multiple_of(at * QUARTER, QUARTER), QUARTER), :], decays[at])
    last_ref[...] = late


def row_kernel(place_ref, own_ref, one_ref, two_ref, three_ref, row_ref, after_ref, reach_ref, held):
    for k, ref in enumerate((own_ref, one_ref, two_ref, three_ref)):
        held[k] = ref[...]
    z = place_ref[2]
    state = jnp.zeros((QUARTER, N), f32)
    decay = jnp.ones((8, N), f32)
    for at in (3, 2, 1, 0):
        after_ref[at] = state
        reach_ref[at] = decay
        here_state, here = quarter_of(held[(at - z) & 3])
        state = here_state + by_head(here[:QUARTER_HEADS]) * state
        decay = here * decay
    put_quarter(row_ref, state, decay)


def end_kernel(place_ref, one_ref, two_ref, three_ref, after_ref, reach_ref, *outs):
    state = jnp.zeros((QUARTER, N), f32)
    for ref in (three_ref, two_ref, one_ref):
        here_state, here = quarter_of(ref[...])
        state = here_state + by_head(here[:QUARTER_HEADS]) * state
    for by, ref in enumerate(outs):
        at = (place_ref[2] + by) & 3
        reach = reach_ref[at]
        ref[...] = (after_ref[at] + by_head(reach[:QUARTER_HEADS]) * state).astype(bf16)


def last_kernel(place_ref, own_ref, one_ref, two_ref, three_ref, last_ref, mine_ref, send_ref, late):
    for by, ref in enumerate((own_ref, one_ref, two_ref, three_ref)):
        at = (place_ref[2] - by) & 3
        late[pl.ds(pl.multiple_of(at * QUARTER, QUARTER), QUARTER), :] = ref[...]
    message = last_ref[...]
    early = (state_of(message) + by_head(decay_of(message)) * late[...].astype(f32)).astype(bf16)
    leads = place_ref[3] == 0
    mine_ref[...] = jnp.where(leads, early, late[...])
    send_ref[...] = jnp.where(leads, late[...], early)


def scan_back_kernel(
    group, x_ref, b_ref, c_ref, run_ref, run_col_ref, dt_col_ref, state_ref, grad_y_ref,
    inner_ref, grad_c_ref, grad_b_ref, row_ref, col_ref, skip_sum_ref,
    scores, back, reads_back, skips,
):
    upper = iota((Q, Q), 0) <= iota((Q, Q), 1)
    skips[...] = jnp.zeros_like(skips)
    col_ref[...] = jnp.zeros_like(col_ref)
    lane = iota((Q, 128), 1)
    keys = b_ref[...]
    reads = c_ref[...]
    scores[...] = dot_rows(keys, reads)
    back[...] = jnp.zeros_like(back)
    reads_back[...] = jnp.zeros_like(reads_back)

    def body(at, carry):
        pair = group * GROUP_PAIRS + at
        lanes = lanes_of(at)
        xs = x_ref[:, lanes].astype(f32)
        grads = grad_y_ref[:, lanes]
        step = dot(dt_col_ref[...], pair_select(pair, P_SIZE))
        scaled = halves((step * xs).astype(bf16))
        split = halves(grads)
        expanded = dot(run_col_ref[...], pair_select(pair, 128))
        top, bottom = [], []
        for k in range(2):
            head = 2 * pair + k
            run_row = run_ref[pl.ds(head, 1), :]
            col = expanded[:, k * 128 : (k + 1) * 128]
            d0 = dot_rows(scaled[k][:Q], grads)
            d11 = dot_rows(scaled[k][Q:], grads[Q:])
            l00 = causal_exp(run_row[:, :Q] - col[:Q], upper)
            l01 = jnp.exp(run_row[:, Q:] - col[:Q])
            l11 = causal_exp(run_row[:, Q:] - col[Q:], upper)
            p00, p01, p11 = l00 * d0[:, :Q], l01 * d0[:, Q:], l11 * d11
            back[:Q, :Q] += p00
            back[:Q, Q:] += p01
            back[Q:, Q:] += p11
            s00, s01, s11 = scores[:Q, :Q], scores[:Q, Q:], scores[Q:, Q:]
            w00, w01, w11 = p00 * s00, p01 * s01, p11 * s11
            row_ref[0, pl.ds(2 * at + k, 1), :] = jnp.sum(w00, axis=0, keepdims=True)
            row_ref[1, pl.ds(2 * at + k, 1), :] = jnp.sum(w01 + w11, axis=0, keepdims=True)
            col_ref[:Q, :] -= jnp.where(lane == head, jnp.sum(w00 + w01, axis=1, keepdims=True), 0.0)
            col_ref[Q:, :] -= jnp.where(lane == head, jnp.sum(w11, axis=1, keepdims=True), 0.0)
            top.extend([(l00 * s00).astype(bf16), (l01 * s01).astype(bf16)])
            bottom.append((l11 * s11).astype(bf16))
        inner_ref[:Q, lanes] = dot(jnp.concatenate(top, axis=1), jnp.concatenate(split, axis=0))
        inner_ref[Q:, lanes] = dot(
            jnp.concatenate(bottom, axis=1),
            jnp.concatenate([split[0][Q:], split[1][Q:]], axis=0),
        )
        state = state_ref[lanes_of(pair), :].astype(bf16)
        first = iota((TOKENS, 128), 1) < P_SIZE
        reach = jnp.exp(jnp.where(first, expanded[:, :128], expanded[:, 128:]))
        wide = grads.astype(f32)
        reached = reach * wide
        reads_back[...] += dot(reached.astype(bf16), state)
        col_ref[...] += pair_sums(reached * dot_rows(reads, state), pair)
        skips[...] += pair_sums(xs * wide, pair)
        return carry

    lax.fori_loop(0, GROUP_PAIRS, body, 0, unroll=UNROLL)
    inner = back[...].astype(bf16)
    grad_b_ref[...] = dot(inner, reads)
    grad_c_ref[...] = (
        dot_columns(inner, keys) + reads_back[...]
    ).astype(bf16)
    skip_sum_ref[...] = jnp.sum(skips[...], axis=0, keepdims=True)


def end_back_kernel(
    place_ref, x_ref, b_ref, dt_ref, rate_ref, skip_ref, run_ref, run_col_ref, dt_col_ref,
    state_ref, mine_ref, got_ref, *refs
):
    per_group, rest = (refs[:8], refs[8:16]), refs[16:]
    end_back_body(
        place_ref, x_ref, b_ref, dt_ref, rate_ref, skip_ref, run_ref, run_col_ref, dt_col_ref,
        state_ref, mine_ref, got_ref, per_group, *rest
    )


def end_back_body(
    place_ref, x_ref, b_ref, dt_ref, rate_ref, skip_ref, run_ref, run_col_ref, dt_col_ref,
    state_ref, mine_ref, got_ref, per_group,
    grad_x_ref, grad_b_ref, grad_dt_ref, grad_start_ref, sums_ref,
    ends, decay, directs, tails, products,
):
    core = place_ref[3]
    ends[pl.ds(pl.multiple_of(core * STATE_ROWS, STATE_ROWS), STATE_ROWS), :] = mine_ref[...]
    ends[pl.ds(pl.multiple_of((1 - core) * STATE_ROWS, STATE_ROWS), STATE_ROWS), :] = got_ref[...]
    run = run_ref[...]
    total = jnp.exp(run[:, TOKENS - 1 : TOKENS])
    decay[...] = jnp.broadcast_to(total, (HEADS, 128))
    directs[...] = jnp.zeros_like(directs)
    tails[...] = jnp.zeros_like(tails)
    for group in range(GROUPS):
        grad_y_ref, inner_ref, keys_back_ref, _, _, _, start_ref, _ = per_group[group]
        keys = b_ref[:, group * N : (group + 1) * N]

        def body(at, keys_back):
            pair = group * GROUP_PAIRS + at
            lanes, local = lanes_of(pair), lanes_of(at)
            end = ends[lanes, :]
            wide_end = end.astype(f32)
            xs = x_ref[:, lanes].astype(f32)
            step = dot(dt_col_ref[...], pair_select(pair, P_SIZE))
            running = dot(run_col_ref[...], pair_select(pair, P_SIZE))
            tail = jnp.exp(running[TOKENS - 1 :, :] - running)
            read = dot_rows(keys, end)
            tailed = tail * (step * xs)
            grad_scaled = inner_ref[:, local] + tail * read
            grad_x = step * grad_scaled + skip_ref[:, lanes] * grad_y_ref[:, local].astype(f32)
            grad_x_ref[:, lanes] = grad_x.astype(bf16)
            directs[...] += pair_sums(xs * grad_scaled, pair)
            tails[...] += pair_sums(tailed * read, pair)
            product = wide_end * state_ref[lanes, :]
            for k in range(2):
                head = 2 * pair + k
                half = slice(k * P_SIZE, (k + 1) * P_SIZE)
                products[pl.ds(head, 1), :] = jnp.sum(product[half], axis=0, keepdims=True)
                rows = pl.ds(pl.multiple_of(head * P_SIZE, P_SIZE), P_SIZE)
                own = pl.ds(pl.multiple_of((2 * at + k) * P_SIZE, P_SIZE), P_SIZE)
                grad_start_ref[rows, :] = start_ref[own, :] + decay[pl.ds(head, 1), :] * wide_end[half]
            return keys_back + dot(tailed.astype(bf16), end)

        keys_back = lax.fori_loop(
            0, GROUP_PAIRS, body, keys_back_ref[...], unroll=UNROLL
        )
        grad_b_ref[:, group * N : (group + 1) * N] = keys_back.astype(bf16)
    tail_rows = tails[...].T[:HEADS]
    shared = jnp.sum(tail_rows, axis=1, keepdims=True)
    shared = shared + total * jnp.sum(products[...], axis=1, keepdims=True)
    rows = [jnp.concatenate([group[3][0], group[3][1]], axis=1) for group in per_group]
    columns = per_group[0][4][...] + per_group[1][4][...] - tails[...]
    here = jnp.concatenate(rows, axis=0) + columns.T[:HEADS]
    since = jnp.where(iota((TOKENS, TOKENS), 0) >= iota((TOKENS, TOKENS), 1), 1.0, 0.0).astype(bf16)
    grad_log = exact_rows(here, since) + shared
    grad_dt = directs[...].T[:HEADS] - rate_ref[...] * grad_log
    spent = -dt_ref[...] * grad_log
    zero = jnp.zeros_like(spent)
    columns = jnp.concatenate([grad_dt, spent, zero, zero], axis=0).T
    grad_dt_ref[...] = columns[:, :HEADS]
    sums = jnp.sum(columns, axis=0, keepdims=True)
    for group in range(GROUPS):
        own = slice(group * GROUP_CHANNELS, (group + 1) * GROUP_CHANNELS)
        sums_ref[:, own] = per_group[group][7][...]
    skips = per_group[0][5][...] + per_group[1][5][...]
    sums_ref[:, CHANNELS:] = jnp.where(iota((1, 128), 1) < HEADS, skips, sums)


def call(kernel, outs, scratch, scalars, *arrays, flops=0, limit=24, after=()):
    specs = [pl.BlockSpec(memory_space=pltpu.SMEM)] * scalars
    plain, size = list(arrays[:scalars]), 0
    for array in arrays[scalars:]:
        array, group = array if isinstance(array, tuple) else (array, None)
        shape = array.shape
        if group is None:
            specs.append(pl.BlockSpec(shape, lambda i, n=len(shape): (0,) * n))
        else:
            shape = shape[:-1] + (shape[-1] // GROUPS,)
            specs.append(pl.BlockSpec(shape, lambda i, group=group: (0, group)))
        size += math.prod(shape) * array.dtype.itemsize
        plain.append(array)
    size += sum(math.prod(shape) * jnp.dtype(kind).itemsize for shape, kind in outs)
    used = len(plain)

    def body(*refs):
        kernel(*refs[:used], *refs[used + len(after) :])

    return pl.pallas_call(
        body,
        grid=(1,),
        out_shape=[jax.ShapeDtypeStruct(shape, kind) for shape, kind in outs],
        in_specs=specs + [pl.BlockSpec(memory_space=pl.ANY)] * len(after),
        out_specs=[pl.BlockSpec(shape, lambda i, n=len(shape): (0,) * n) for shape, _ in outs],
        scratch_shapes=[pltpu.VMEM(shape, kind) for shape, kind in scratch],
        name=getattr(kernel, "func", kernel).__name__,
        compiler_params=pltpu.CompilerParams(vmem_limit_bytes=limit * 2**20),
        cost_estimate=pl.CostEstimate(flops=flops, bytes_accessed=size, transcendentals=0),
    )(*plain, *after)


WIDE = (TOKENS, GROUP_CHANNELS)


def prepare(place, dout, steps, rate):
    return call(
        prepare_kernel,
        [((TOKENS, 512), bf16)] * 2
        + [((HEADS, TOKENS), f32), ((TOKENS, 128), bf16), ((TOKENS, 128), bf16)],
        [], 1, place, dout, steps, rate,
    )


def forward(group, x, z, b, c, steps, run, run_col, state, gain, skip, after):
    return call(
        functools.partial(forward_kernel, group),
        [(WIDE, f32), (WIDE, bf16)],
        [((TOKENS, TOKENS), f32), (WIDE, f32), ((TOKENS, 128), f32)],
        0, (x, group), (z, group), (b, group), (c, group), steps, run, run_col,
        state, (gain, group), (skip, group), flops=SHORT, after=after,
    )


MESSAGE = ((STATE_ROWS + 2 * PER_GROUP, N), bf16)


def norm_back(group, place, own, other, y, z, c, gain, run, run_col, first, after):
    outs = [(WIDE, bf16), (WIDE, bf16), ((1, GROUP_CHANNELS), f32), ((STATE_ROWS, N), f32), MESSAGE]
    return call(
        functools.partial(norm_back_kernel, group),
        outs + ([MESSAGE] if group else []),
        [((TOKENS, 128), f32), ((TOKENS, 128), f32)],
        1, place, own, other, y, (z, group), (c, group), (gain, group), run, run_col, *first,
        flops=LONG, after=after,
    )


PART = ((QUARTER + 16, N), bf16)


def chip_state(place, keep, got):
    return call(
        chip_kernel, [PART] * 4 + [MESSAGE], [((STATE_ROWS, N), f32), ((4, 8, N), f32)],
        1, place, keep, got,
    )


def row_state(place, own, one, two, three, after):
    return call(
        row_kernel, [PART, ((4, QUARTER, N), f32), ((4, 8, N), f32)],
        [((4, QUARTER + 16, N), bf16)], 1, place, own, one, two, three, after=after,
    )


def end_state(place, one, two, three, follows, reach, after):
    return call(
        end_kernel, [((QUARTER, N), bf16)] * 4, [], 1, place, one, two, three, follows, reach,
        after=after,
    )


def last_state(place, own, one, two, three, last):
    return call(
        last_kernel, [((STATE_ROWS, N), bf16)] * 2, [((STATE_ROWS, N), bf16)],
        1, place, own, one, two, three, last,
    )


def scan_back(group, x, b, c, run, run_col, dt_col, state, grad_y, after):
    return call(
        functools.partial(scan_back_kernel, group),
        [(WIDE, f32), ((TOKENS, N), bf16), ((TOKENS, N), f32), ((2, PER_GROUP, Q), f32),
         ((TOKENS, 128), f32), ((1, 128), f32)],
        [((TOKENS, TOKENS), f32), ((TOKENS, TOKENS), f32), ((TOKENS, N), f32), ((TOKENS, 128), f32)],
        0, (x, group), (b, group), (c, group), run, run_col, dt_col, state, grad_y,
        flops=LONG, after=after,
    )


def end_back(place, *arrays, after):
    return call(
        end_back_kernel,
        [((TOKENS, CHANNELS), bf16), ((TOKENS, GROUPS * N), bf16), ((TOKENS, HEADS), f32),
         ((CHANNELS, N), f32), ((1, CHANNELS + 128), f32)],
        [((CHANNELS, N), bf16), ((HEADS, 128), f32), ((TOKENS, 128), f32), ((TOKENS, 128), f32),
         ((HEADS, 128), f32)],
        1, place, *arrays, flops=LONG, limit=32, after=after,
    )


HALF = CHANNELS // 2
TILE = 512


def turn_kernel(place_ref, own_ref, before_ref, after_ref, far0_ref, far1_ref, pieces_ref, turned_ref):
    far = jnp.concatenate([far0_ref[...], far1_ref[...]], axis=0)
    for by, piece in ((0, own_ref[...]), (-1, before_ref[...]), (1, after_ref[...]), (2, far)):
        at = (place_ref[0] + by) & 3
        rows = pl.ds(pl.multiple_of(at * 512, 512), 512)
        pieces_ref[rows, :] = piece
        turned_ref[rows, :] = piece.T


def turn(place, *pieces, after):
    return call(
        turn_kernel, [((2048, 512), bf16)] * 2, [], 1, place, *pieces, flops=SHORT, after=after
    )


def weight_grad_kernel(turned_ref, own0_ref, other0_ref, own1_ref, other1_ref, out_ref):
    first = pl.program_id(0) < HALF // TILE
    own = jnp.where(first, own0_ref[...], own1_ref[...])
    other = jnp.where(first, other0_ref[...], other1_ref[...])
    right = jnp.concatenate([own, other], axis=0)
    for at in range(0, 2048, 512):
        out_ref[at : at + 512, :] = dot(turned_ref[at : at + 512, :], right).astype(bf16)


def weight_grad(turned, *normed):
    last = HALF // TILE - 1
    early = pl.BlockSpec((TOKENS, TILE), lambda i: (0, jnp.minimum(i, last)))
    late = pl.BlockSpec((TOKENS, TILE), lambda i: (0, jnp.maximum(i - last - 1, 0)))
    return pl.pallas_call(
        weight_grad_kernel,
        name="weight_grad",
        grid=(CHANNELS // TILE,),
        out_shape=jax.ShapeDtypeStruct((2048, CHANNELS), bf16),
        in_specs=[pl.BlockSpec((2048, 512), lambda i: (0, 0)), early, early, late, late],
        out_specs=pl.BlockSpec((2048, TILE), lambda i: (0, i)),
        compiler_params=pltpu.CompilerParams(vmem_limit_bytes=24 * 2**20),
        cost_estimate=pl.CostEstimate(flops=SHORT, bytes_accessed=1024, transcendentals=0),
    )(turned, *normed)


def upstream_whole_kernel(half, place_ref, pieces_ref, weight_ref, *refs):
    own_ref, other_ref = refs[-2:]
    total = None
    for at in range(0, 2048, 512):
        product = dot(pieces_ref[at : at + 512, :], weight_ref[at : at + 512, :])
        total = product if total is None else total + product
    own_ref[...] = total[:TOKENS]
    other_ref[...] = total[TOKENS:].astype(bf16)


def upstream(kernel, half, place, pieces, arrays, outs, after):
    return pl.pallas_call(
        functools.partial(kernel, half),
        name=f"{kernel.__name__}_{half}",
        grid=(HALF // TILE,),
        out_shape=[jax.ShapeDtypeStruct((rows, HALF), kind) for rows, kind in outs],
        in_specs=[pl.BlockSpec(memory_space=pltpu.SMEM), pl.BlockSpec((2048, 512), lambda i: (0, 0))]
        + [pl.BlockSpec((a.shape[0], TILE), lambda i: (0, half * (HALF // TILE) + i)) for a in arrays]
        + [pl.BlockSpec(memory_space=pl.ANY)] * len(after),
        out_specs=[pl.BlockSpec((rows, TILE), lambda i: (0, i)) for rows, _ in outs],
        compiler_params=pltpu.CompilerParams(vmem_limit_bytes=24 * 2**20),
        cost_estimate=pl.CostEstimate(flops=SHORT, bytes_accessed=1024, transcendentals=0),
    )(place, pieces, *arrays, *after)


def upstream_whole(half, place, pieces, weights, after):
    outs = [(TOKENS, f32), (TOKENS, bf16)]
    return upstream(upstream_whole_kernel, half, place, pieces, (weights,), outs, after)


def device(y, z, core):
    return (y * 4 + z) * 2 + core


PLACES = [(y, z, core) for y in range(4) for z in range(4) for core in range(2)]
SAME_CORE = [[device(y, z, core) for y in range(4) for z in range(4)] for core in range(2)]
SWAP = [(device(y, z, core), device(y, z, 1 - core)) for y, z, core in PLACES]


def along_z(by):
    return [(device(y, z, core), device(y, (z + by) % 4, core)) for y, z, core in PLACES]


def along_y(by):
    return [(device(y, z, core), device((y + by) % 4, z, core)) for y, z, core in PLACES]


def earlier_y(by):
    return [(device(y, z, core), device(y - by, z, core)) for y, z, core in PLACES if y >= by]


def move(array, pairs):
    return lax.ppermute(array, "ctx", pairs)


def along_x(array, by):
    return lax.ppermute(array, "head", [(x, (x + by) % 4) for x in range(4)])


def sum_ctx(array):
    array = array + move(array, SWAP)
    array = array + move(array, along_z(1)) + move(array, along_z(2)) + move(array, along_z(3))
    return array + move(array, along_y(1)) + move(array, along_y(2)) + move(array, along_y(3))


def per_device(dout, out_weight, x_in, z_in, b_in, c_in, dt, rate, skip, gain, start_state):
    at = lax.axis_index("ctx")
    place = jnp.stack([lax.axis_index("head"), at // 8, (at // 2) % 4, at % 2]).astype(jnp.int32)
    steps = dt.T
    rates = rate.reshape(HEADS, 1)
    skips = jnp.repeat(skip, P_SIZE).reshape(1, CHANNELS)
    gains = gain.reshape(1, CHANNELS)
    state = start_state.reshape(CHANNELS, N)
    weights = lax.all_gather(out_weight, "ctx", axis=0, tiled=True, axis_index_groups=SAME_CORE)
    keep, send, run, run_col, dt_col = prepare(place, dout, steps, rates)
    both = jnp.concatenate([keep, move(send, SWAP)], axis=0)
    x_before, x_after = along_x(both, 1), along_x(both, -1)
    scan_in = (x_in, z_in, b_in, c_in, steps, run, run_col, state, gains, skips)
    y0, normed0 = forward(0, *scan_in, (both,))
    y1, normed1 = forward(1, *scan_in, (normed0, x_before, x_after))
    x_far = along_x(x_before[:TOKENS], 1), along_x(x_after[TOKENS:], -1)
    other0, other1 = move(normed0, SWAP), move(normed1, SWAP)
    pieces, turned = turn(place, both, x_before, x_after, *x_far, after=(normed1,))
    term = weight_grad(turned, normed0, other0, normed1, other1)
    grad_w = lax.psum_scatter(
        term, "ctx", scatter_dimension=0, tiled=True, axis_index_groups=SAME_CORE
    )
    part0, send0 = upstream_whole(0, place, pieces, weights, (term,))
    part1, send1 = upstream_whole(1, place, pieces, weights, (part0,))
    back_in = (z_in, c_in, gains, run, run_col)
    grad_y0, grad_z0, gain_sum0, start0, message0 = norm_back(
        0, place, part0, move(send0, SWAP), y0, *back_in, (), (part1,)
    )
    grad_y1, grad_z1, gain_sum1, start1, keep, send = norm_back(
        1, place, part1, move(send1, SWAP), y1, *back_in, (message0,), (grad_y0,)
    )
    *quarters, last = chip_state(place, keep, move(send, SWAP))
    from_z = [move(quarters[-k], along_z(-k)) for k in (1, 2, 3)]
    back0 = scan_back(
        0, x_in, b_in, c_in, run, run_col, dt_col, state, grad_y0, (quarters[0],)
    )
    row, after, reach = row_state(place, quarters[0], *from_z, after=(back0[0],))
    from_y = [move(row, earlier_y(k)) for k in (1, 2, 3)]
    back1 = scan_back(
        1, x_in, b_in, c_in, run, run_col, dt_col, state, grad_y1, (row,)
    )
    ends = end_state(place, *from_y, after, reach, after=(back1[0],))
    mine, theirs = last_state(place, ends[0], *[move(ends[k], along_z(k)) for k in (1, 2, 3)], last)
    grad_x, grad_b, grad_dt, grad_start, sums = end_back(
        place, x_in, b_in, steps, rates, skips, run, run_col, dt_col, state, mine,
        move(theirs, SWAP),
        grad_y0, *[back0[i] for i in (0, 2, 3, 4, 5)], start0, gain_sum0,
        grad_y1, *[back1[i] for i in (0, 2, 3, 4, 5)], start1, gain_sum1,
        after=(),
    )
    sums = sum_ctx(sums)[0]
    return (
        grad_x,
        jnp.concatenate([grad_z0, grad_z1], axis=1),
        grad_b,
        jnp.concatenate([back0[1], back1[1]], axis=1),
        grad_dt,
        grad_w,
        sums[:CHANNELS],
        sums[CHANNELS + HEADS : CHANNELS + 2 * HEADS],
        sums[CHANNELS : CHANNELS + HEADS],
        grad_start.reshape(start_state.shape),
    )


def solution(mesh):
    full, whole = P("ctx", "head"), P("head")
    state = P("ctx", "head", None, None)
    return jax.shard_map(
        per_device,
        mesh=mesh,
        in_specs=(full,) * 7 + (whole,) * 3 + (state,),
        out_specs=(full,) * 6 + (whole,) * 3 + (state,),
        check_vma=False,
    )
```

```python
import functools
import math

import jax
import jax.numpy as jnp
from jax import lax
from jax.experimental import pallas as pl
from jax.experimental.pallas import tpu as pltpu
from jax.sharding import PartitionSpec as P

P_SIZE = 64
N = 128
Q = 128
TOKENS = 256
HEADS = 32
GROUPS = 2
PER_GROUP = HEADS // GROUPS
CHANNELS = HEADS * P_SIZE
GROUP_CHANNELS = PER_GROUP * P_SIZE
PAIRS = HEADS // 2
GROUP_PAIRS = PER_GROUP // 2
STATE_ROWS = PER_GROUP * P_SIZE
EPSILON = 1e-05
UNROLL = 4
SHORT, LONG = 100000000, 28000000000

f32 = jnp.float32
bf16 = jnp.bfloat16


def dot(a, b, over=((1,), (0,))):
    return lax.dot_general(a, b, (over, ((), ())), preferred_element_type=f32)


def dot_rows(a, b):
    return dot(a, b, ((1,), (1,)))


def dot_columns(a, b):
    return dot(a, b, ((0,), (0,)))


def iota(shape, axis):
    return lax.broadcasted_iota(jnp.int32, shape, axis)


def split2(v):
    high = v.astype(bf16)
    return high, (v - high.astype(f32)).astype(bf16)


def split3(v):
    high = v.astype(bf16)
    rest = v - high.astype(f32)
    middle = rest.astype(bf16)
    return high, middle, (rest - middle.astype(f32)).astype(bf16)


def exact_rows(rows, right):
    product = dot(jnp.concatenate(split3(rows), axis=0), right)
    return product[:HEADS] + product[HEADS : 2 * HEADS] + product[2 * HEADS :]


def part_columns(rows):
    parts = [part.astype(f32) for part in split3(rows)]
    stacked = jnp.concatenate(parts + [jnp.zeros_like(rows)], axis=0)
    return stacked.T.astype(bf16)


def pair_select(pair, width):
    row = iota((128, 2 * width), 0)
    head = 2 * pair + jnp.where(iota((128, 2 * width), 1) >= width, 1, 0)
    hit = ((row & (HEADS - 1)) == head) & (row < 3 * HEADS)
    return jnp.where(hit, 1.0, 0.0).astype(bf16)


def pair_sums(values, pair):
    row, lane = iota((128, 128), 0), iota((128, 128), 1)
    head = 2 * pair + jnp.where(row >= P_SIZE, 1, 0)
    place = jnp.where(lane == head, 1.0, 0.0).astype(bf16)
    high, low = split2(values)
    return dot(jnp.concatenate([high, low], axis=1), jnp.concatenate([place, place], axis=0))


def lanes_of(pair):
    return pl.ds(pl.multiple_of(pair * 128, 128), 128)


def halves(v):
    first = iota(v.shape, 1) < P_SIZE
    zero = jnp.zeros_like(v)
    return jnp.where(first, v, zero), jnp.where(first, zero, v)


def causal_exp(spread, keep):
    return jnp.exp(jnp.where(keep, spread, -1e30))


def prepare_kernel(place_ref, dout_ref, dt_ref, rate_ref, keep_ref, send_ref, run_ref, run_col_ref, dt_col_ref):
    leads = place_ref[3] == 0
    for at in range(4):
        even = dout_ref[:, 256 * at : 256 * at + 128]
        odd = dout_ref[:, 256 * at + 128 : 256 * at + 256]
        own = slice(128 * at, 128 * at + 128)
        keep_ref[:, own] = jnp.where(leads, even, odd)
        send_ref[:, own] = jnp.where(leads, odd, even)
    steps = dt_ref[...]
    upto = jnp.where(iota((TOKENS, TOKENS), 0) <= iota((TOKENS, TOKENS), 1), 1.0, 0.0).astype(bf16)
    run = exact_rows(-steps * rate_ref[...], upto)
    run_ref[...] = run
    run_col_ref[...] = part_columns(run)
    dt_col_ref[...] = part_columns(steps)


def forward_kernel(
    x_ref, z_ref, b_ref, c_ref, dt_ref, run_ref, run_col_ref, state_ref, gain_ref, skip_ref,
    y_ref, normed_ref,
    scores, gated_ref, power,
):
    group = pl.program_id(0)
    lower = iota((Q, Q), 0) >= iota((Q, Q), 1)
    reads = c_ref[...]
    scores[...] = dot_rows(reads, b_ref[...])
    power[...] = jnp.zeros_like(power)

    def body(at, carry):
        pair = group * GROUP_PAIRS + at
        lanes = own = lanes_of(at)
        xs = x_ref[:, lanes]
        expanded = dot(run_col_ref[...], pair_select(pair, 128))
        top, bottom = [], []
        for k in range(2):
            run_row = run_ref[pl.ds(2 * pair + k, 1), :]
            dt_row = dt_ref[pl.ds(2 * pair + k, 1), :]
            col = expanded[:, k * 128 : (k + 1) * 128]
            m00 = causal_exp(col[:Q] - run_row[:, :Q], lower) * (scores[:Q, :Q] * dt_row[:, :Q])
            m10 = jnp.exp(col[Q:] - run_row[:, :Q]) * (scores[Q:, :Q] * dt_row[:, :Q])
            m11 = causal_exp(col[Q:] - run_row[:, Q:], lower) * (scores[Q:, Q:] * dt_row[:, Q:])
            top.append(m00.astype(bf16))
            bottom.extend([m10.astype(bf16), m11.astype(bf16)])
        x0, x1 = halves(xs)
        y0 = dot(jnp.concatenate(top, axis=1), jnp.concatenate([x0[:Q], x1[:Q]], axis=0))
        y1 = dot(jnp.concatenate(bottom, axis=1), jnp.concatenate([x0, x1], axis=0))
        from_start = dot_rows(reads, state_ref[lanes_of(at), :].astype(bf16))
        first = iota((TOKENS, 128), 1) < P_SIZE
        reach = jnp.exp(jnp.where(first, expanded[:, :128], expanded[:, 128:]))
        y = jnp.concatenate([y0, y1], axis=0) + reach * from_start
        y = y + skip_ref[:, lanes] * xs.astype(f32)
        y_ref[:, lanes] = y
        gate = z_ref[:, lanes].astype(f32)
        gated = y * gate / (1.0 + jnp.exp(-gate))
        gated_ref[:, own] = gated
        power[...] += gated * gated
        return carry

    lax.fori_loop(0, GROUP_PAIRS, body, 0, unroll=UNROLL)
    mean = jnp.sum(power[...], axis=1, keepdims=True) * (1.0 / GROUP_CHANNELS)
    scale = jnp.broadcast_to(lax.rsqrt(mean + EPSILON), (TOKENS, 128))

    def finish(at, carry):
        lanes = own = lanes_of(at)
        normed_ref[:, lanes] = (gated_ref[:, own] * scale * gain_ref[:, lanes]).astype(bf16)
        return carry

    lax.fori_loop(0, GROUP_PAIRS, finish, 0, unroll=UNROLL)


def norm_back_kernel(
    group, place_ref, own_ref, other_ref, y_ref, z_ref, c_ref, gain_ref, run_ref, run_col_ref, *rest
):
    first_ref, rest = (rest[0], rest[1:]) if group else (None, rest)
    grad_y_ref, grad_z_ref, gain_sum_ref, start_ref = rest[:4]
    outs, (power, along) = rest[4:-2], rest[-2:]
    reads = c_ref[...]
    power[...] = jnp.zeros_like(power)
    along[...] = jnp.zeros_like(along)

    def pieces(at):
        lanes = lanes_of(at)
        upstream = own_ref[:, lanes] + other_ref[:, lanes].astype(f32)
        gate = z_ref[:, lanes].astype(f32)
        sigmoid = 1.0 / (1.0 + jnp.exp(-gate))
        y = y_ref[:, lanes]
        return lanes, upstream, gate, sigmoid, y, y * gate * sigmoid

    def first(at, carry):
        lanes, upstream, gate, sigmoid, y, gated = pieces(at)
        power[...] += gated * gated
        along[...] += upstream * gain_ref[:, lanes] * gated
        return carry

    lax.fori_loop(0, GROUP_PAIRS, first, 0, unroll=UNROLL)
    mean = jnp.sum(power[...], axis=1, keepdims=True) * (1.0 / GROUP_CHANNELS)
    scale = lax.rsqrt(mean + EPSILON)
    shared = jnp.sum(along[...], axis=1, keepdims=True) * (1.0 / GROUP_CHANNELS)
    pull = jnp.broadcast_to(scale * scale * scale * shared, (TOKENS, 128))
    scale = jnp.broadcast_to(scale, (TOKENS, 128))

    def second(at, carry):
        lanes, upstream, gate, sigmoid, y, gated = pieces(at)
        grad_gated = scale * (upstream * gain_ref[:, lanes]) - gated * pull
        grad_y = grad_gated * (gate * sigmoid)
        grad_y_ref[:, lanes] = grad_y.astype(bf16)
        slope = sigmoid * (1.0 + gate * (1.0 - sigmoid))
        grad_z_ref[:, lanes] = (grad_gated * y * slope).astype(bf16)
        gain_sum_ref[:, lanes] = jnp.sum(upstream * gated * scale, axis=0, keepdims=True)
        pair = group * GROUP_PAIRS + at
        reach = jnp.exp(dot(run_col_ref[...], pair_select(pair, P_SIZE)))
        start_ref[lanes, :] = dot_columns((grad_y * reach).astype(bf16), reads)
        return carry

    lax.fori_loop(0, GROUP_PAIRS, second, 0, unroll=UNROLL)
    total = jnp.exp(run_ref[group * PER_GROUP : (group + 1) * PER_GROUP, TOKENS - 1 :])
    high, low = split2(jnp.broadcast_to(total, (PER_GROUP, 128)))
    states = start_ref[...].astype(bf16)
    if first_ref is None:
        ref = outs[0]
        ref[:STATE_ROWS, :] = states
        ref[STATE_ROWS : STATE_ROWS + PER_GROUP, :] = high
        ref[STATE_ROWS + PER_GROUP :, :] = low
    else:
        message = jnp.concatenate([states, high, low], axis=0)
        leads = place_ref[3] == 0
        outs[0][...] = jnp.where(leads, first_ref[...], message)
        outs[1][...] = jnp.where(leads, message, first_ref[...])


QUARTER = STATE_ROWS // 4
QUARTER_HEADS = PER_GROUP // 4


def by_head(decay):
    heads = decay.shape[0]
    return jnp.broadcast_to(decay[:, None, :], (heads, P_SIZE, N)).reshape(heads * P_SIZE, N)


def decay_of(message):
    first = message[STATE_ROWS : STATE_ROWS + PER_GROUP, :].astype(f32)
    return first + message[STATE_ROWS + PER_GROUP :, :].astype(f32)


def state_of(message):
    return message[:STATE_ROWS, :].astype(f32)


def put_quarter(ref, state, decay):
    ref[:QUARTER, :] = state.astype(bf16)
    high, low = split2(decay)
    ref[QUARTER:, :] = jnp.concatenate([high.astype(f32), low.astype(f32)], axis=0).astype(bf16)


def quarter_of(message):
    decay = message[QUARTER:, :].astype(f32)
    return message[:QUARTER, :].astype(f32), decay[:8] + decay[8:]


def chip_kernel(place_ref, keep_ref, got_ref, *refs):
    outs, last_ref, states, decays = refs[:4], refs[4], refs[5], refs[6]
    leads = place_ref[3] == 0
    keep, got = keep_ref[...], got_ref[...]
    early, late = jnp.where(leads, keep, got), jnp.where(leads, got, keep)
    decay = decay_of(early)
    states[...] = state_of(early) + by_head(decay) * state_of(late)
    decay = decay * decay_of(late)
    decays[...] = jnp.zeros_like(decays)
    for at in range(4):
        decays[at, :QUARTER_HEADS, :] = decay[at * QUARTER_HEADS : (at + 1) * QUARTER_HEADS]
    for by, ref in enumerate(outs):
        at = (place_ref[2] + by) & 3
        put_quarter(ref, states[pl.ds(pl.multiple_of(at * QUARTER, QUARTER), QUARTER), :], decays[at])
    last_ref[...] = late


def row_kernel(place_ref, own_ref, one_ref, two_ref, three_ref, row_ref, after_ref, reach_ref, held):
    for k, ref in enumerate((own_ref, one_ref, two_ref, three_ref)):
        held[k] = ref[...]
    z = place_ref[2]
    state = jnp.zeros((QUARTER, N), f32)
    decay = jnp.ones((8, N), f32)
    for at in (3, 2, 1, 0):
        after_ref[at] = state
        reach_ref[at] = decay
        here_state, here = quarter_of(held[(at - z) & 3])
        state = here_state + by_head(here[:QUARTER_HEADS]) * state
        decay = here * decay
    put_quarter(row_ref, state, decay)


def end_kernel(place_ref, one_ref, two_ref, three_ref, after_ref, reach_ref, *outs):
    state = jnp.zeros((QUARTER, N), f32)
    for ref in (three_ref, two_ref, one_ref):
        here_state, here = quarter_of(ref[...])
        state = here_state + by_head(here[:QUARTER_HEADS]) * state
    for by, ref in enumerate(outs):
        at = (place_ref[2] + by) & 3
        reach = reach_ref[at]
        ref[...] = (after_ref[at] + by_head(reach[:QUARTER_HEADS]) * state).astype(bf16)


def last_kernel(place_ref, own_ref, one_ref, two_ref, three_ref, last_ref, mine_ref, send_ref, late):
    for by, ref in enumerate((own_ref, one_ref, two_ref, three_ref)):
        at = (place_ref[2] - by) & 3
        late[pl.ds(pl.multiple_of(at * QUARTER, QUARTER), QUARTER), :] = ref[...]
    message = last_ref[...]
    early = (state_of(message) + by_head(decay_of(message)) * late[...].astype(f32)).astype(bf16)
    leads = place_ref[3] == 0
    mine_ref[...] = jnp.where(leads, early, late[...])
    send_ref[...] = jnp.where(leads, late[...], early)


def scan_back_kernel(
    group, x_ref, b_ref, c_ref, run_ref, run_col_ref, dt_col_ref, state_ref, grad_y_ref,
    inner_ref, grad_c_ref, grad_b_ref, row_ref, col_ref, skip_sum_ref,
    scores, back, reads_back, skips,
):
    upper = iota((Q, Q), 0) <= iota((Q, Q), 1)
    skips[...] = jnp.zeros_like(skips)
    col_ref[...] = jnp.zeros_like(col_ref)
    lane = iota((Q, 128), 1)
    keys = b_ref[...]
    reads = c_ref[...]
    scores[...] = dot_rows(keys, reads)
    back[...] = jnp.zeros_like(back)
    reads_back[...] = jnp.zeros_like(reads_back)

    def body(at, carry):
        pair = group * GROUP_PAIRS + at
        lanes = lanes_of(at)
        xs = x_ref[:, lanes].astype(f32)
        grads = grad_y_ref[:, lanes]
        step = dot(dt_col_ref[...], pair_select(pair, P_SIZE))
        scaled = halves((step * xs).astype(bf16))
        split = halves(grads)
        expanded = dot(run_col_ref[...], pair_select(pair, 128))
        top, bottom = [], []
        for k in range(2):
            head = 2 * pair + k
            run_row = run_ref[pl.ds(head, 1), :]
            col = expanded[:, k * 128 : (k + 1) * 128]
            d0 = dot_rows(scaled[k][:Q], grads)
            d11 = dot_rows(scaled[k][Q:], grads[Q:])
            l00 = causal_exp(run_row[:, :Q] - col[:Q], upper)
            l01 = jnp.exp(run_row[:, Q:] - col[:Q])
            l11 = causal_exp(run_row[:, Q:] - col[Q:], upper)
            p00, p01, p11 = l00 * d0[:, :Q], l01 * d0[:, Q:], l11 * d11
            back[:Q, :Q] += p00
            back[:Q, Q:] += p01
            back[Q:, Q:] += p11
            s00, s01, s11 = scores[:Q, :Q], scores[:Q, Q:], scores[Q:, Q:]
            w00, w01, w11 = p00 * s00, p01 * s01, p11 * s11
            row_ref[0, pl.ds(2 * at + k, 1), :] = jnp.sum(w00, axis=0, keepdims=True)
            row_ref[1, pl.ds(2 * at + k, 1), :] = jnp.sum(w01 + w11, axis=0, keepdims=True)
            col_ref[:Q, :] -= jnp.where(lane == head, jnp.sum(w00 + w01, axis=1, keepdims=True), 0.0)
            col_ref[Q:, :] -= jnp.where(lane == head, jnp.sum(w11, axis=1, keepdims=True), 0.0)
            top.extend([(l00 * s00).astype(bf16), (l01 * s01).astype(bf16)])
            bottom.append((l11 * s11).astype(bf16))
        inner_ref[:Q, lanes] = dot(jnp.concatenate(top, axis=1), jnp.concatenate(split, axis=0))
        inner_ref[Q:, lanes] = dot(
            jnp.concatenate(bottom, axis=1),
            jnp.concatenate([split[0][Q:], split[1][Q:]], axis=0),
        )
        state = state_ref[lanes_of(pair), :].astype(bf16)
        first = iota((TOKENS, 128), 1) < P_SIZE
        reach = jnp.exp(jnp.where(first, expanded[:, :128], expanded[:, 128:]))
        wide = grads.astype(f32)
        reached = reach * wide
        reads_back[...] += dot(reached.astype(bf16), state)
        col_ref[...] += pair_sums(reached * dot_rows(reads, state), pair)
        skips[...] += pair_sums(xs * wide, pair)
        return carry

    lax.fori_loop(0, GROUP_PAIRS, body, 0, unroll=UNROLL)
    inner = back[...].astype(bf16)
    grad_b_ref[...] = dot(inner, reads)
    grad_c_ref[...] = (
        dot_columns(inner, keys) + reads_back[...]
    ).astype(bf16)
    skip_sum_ref[...] = jnp.sum(skips[...], axis=0, keepdims=True)


def end_back_kernel(
    place_ref, x_ref, b_ref, dt_ref, rate_ref, skip_ref, run_ref, run_col_ref, dt_col_ref,
    state_ref, mine_ref, got_ref, *refs
):
    per_group, rest = (refs[:8], refs[8:16]), refs[16:]
    end_back_body(
        place_ref, x_ref, b_ref, dt_ref, rate_ref, skip_ref, run_ref, run_col_ref, dt_col_ref,
        state_ref, mine_ref, got_ref, per_group, *rest
    )


def end_back_body(
    place_ref, x_ref, b_ref, dt_ref, rate_ref, skip_ref, run_ref, run_col_ref, dt_col_ref,
    state_ref, mine_ref, got_ref, per_group,
    grad_x_ref, grad_b_ref, grad_dt_ref, grad_start_ref, sums_ref,
    ends, decay, directs, tails, products,
):
    core = place_ref[3]
    ends[pl.ds(pl.multiple_of(core * STATE_ROWS, STATE_ROWS), STATE_ROWS), :] = mine_ref[...]
    ends[pl.ds(pl.multiple_of((1 - core) * STATE_ROWS, STATE_ROWS), STATE_ROWS), :] = got_ref[...]
    run = run_ref[...]
    total = jnp.exp(run[:, TOKENS - 1 : TOKENS])
    decay[...] = jnp.broadcast_to(total, (HEADS, 128))
    directs[...] = jnp.zeros_like(directs)
    tails[...] = jnp.zeros_like(tails)
    for group in range(GROUPS):
        grad_y_ref, inner_ref, keys_back_ref, _, _, _, start_ref, _ = per_group[group]
        keys = b_ref[:, group * N : (group + 1) * N]

        def body(at, keys_back):
            pair = group * GROUP_PAIRS + at
            lanes, local = lanes_of(pair), lanes_of(at)
            end = ends[lanes, :]
            wide_end = end.astype(f32)
            xs = x_ref[:, lanes].astype(f32)
            step = dot(dt_col_ref[...], pair_select(pair, P_SIZE))
            running = dot(run_col_ref[...], pair_select(pair, P_SIZE))
            tail = jnp.exp(running[TOKENS - 1 :, :] - running)
            read = dot_rows(keys, end)
            tailed = tail * (step * xs)
            grad_scaled = inner_ref[:, local] + tail * read
            grad_x = step * grad_scaled + skip_ref[:, lanes] * grad_y_ref[:, local].astype(f32)
            grad_x_ref[:, lanes] = grad_x.astype(bf16)
            directs[...] += pair_sums(xs * grad_scaled, pair)
            tails[...] += pair_sums(tailed * read, pair)
            product = wide_end * state_ref[lanes, :]
            for k in range(2):
                head = 2 * pair + k
                half = slice(k * P_SIZE, (k + 1) * P_SIZE)
                products[pl.ds(head, 1), :] = jnp.sum(product[half], axis=0, keepdims=True)
                rows = pl.ds(pl.multiple_of(head * P_SIZE, P_SIZE), P_SIZE)
                own = pl.ds(pl.multiple_of((2 * at + k) * P_SIZE, P_SIZE), P_SIZE)
                grad_start_ref[rows, :] = start_ref[own, :] + decay[pl.ds(head, 1), :] * wide_end[half]
            return keys_back + dot(tailed.astype(bf16), end)

        keys_back = lax.fori_loop(
            0, GROUP_PAIRS, body, keys_back_ref[...], unroll=UNROLL
        )
        grad_b_ref[:, group * N : (group + 1) * N] = keys_back.astype(bf16)
    tail_rows = tails[...].T[:HEADS]
    shared = jnp.sum(tail_rows, axis=1, keepdims=True)
    shared = shared + total * jnp.sum(products[...], axis=1, keepdims=True)
    rows = [jnp.concatenate([group[3][0], group[3][1]], axis=1) for group in per_group]
    columns = per_group[0][4][...] + per_group[1][4][...] - tails[...]
    here = jnp.concatenate(rows, axis=0) + columns.T[:HEADS]
    since = jnp.where(iota((TOKENS, TOKENS), 0) >= iota((TOKENS, TOKENS), 1), 1.0, 0.0).astype(bf16)
    grad_log = exact_rows(here, since) + shared
    grad_dt = directs[...].T[:HEADS] - rate_ref[...] * grad_log
    spent = -dt_ref[...] * grad_log
    zero = jnp.zeros_like(spent)
    columns = jnp.concatenate([grad_dt, spent, zero, zero], axis=0).T
    grad_dt_ref[...] = columns[:, :HEADS]
    sums = jnp.sum(columns, axis=0, keepdims=True)
    for group in range(GROUPS):
        own = slice(group * GROUP_CHANNELS, (group + 1) * GROUP_CHANNELS)
        sums_ref[:, own] = per_group[group][7][...]
    skips = per_group[0][5][...] + per_group[1][5][...]
    sums_ref[:, CHANNELS:] = jnp.where(iota((1, 128), 1) < HEADS, skips, sums)


def call(kernel, outs, scratch, scalars, *arrays, flops=0, limit=24, after=()):
    specs = [pl.BlockSpec(memory_space=pltpu.SMEM)] * scalars
    plain, size = list(arrays[:scalars]), 0
    for array in arrays[scalars:]:
        array, group = array if isinstance(array, tuple) else (array, None)
        shape = array.shape
        if group is None:
            specs.append(pl.BlockSpec(shape, lambda i, n=len(shape): (0,) * n))
        else:
            shape = shape[:-1] + (shape[-1] // GROUPS,)
            specs.append(pl.BlockSpec(shape, lambda i, group=group: (0, group)))
        size += math.prod(shape) * array.dtype.itemsize
        plain.append(array)
    size += sum(math.prod(shape) * jnp.dtype(kind).itemsize for shape, kind in outs)
    used = len(plain)

    def body(*refs):
        kernel(*refs[:used], *refs[used + len(after) :])

    return pl.pallas_call(
        body,
        grid=(1,),
        out_shape=[jax.ShapeDtypeStruct(shape, kind) for shape, kind in outs],
        in_specs=specs + [pl.BlockSpec(memory_space=pl.ANY)] * len(after),
        out_specs=[pl.BlockSpec(shape, lambda i, n=len(shape): (0,) * n) for shape, _ in outs],
        scratch_shapes=[pltpu.VMEM(shape, kind) for shape, kind in scratch],
        name=getattr(kernel, "func", kernel).__name__,
        compiler_params=pltpu.CompilerParams(vmem_limit_bytes=limit * 2**20),
        cost_estimate=pl.CostEstimate(flops=flops, bytes_accessed=size, transcendentals=0),
    )(*plain, *after)


WIDE = (TOKENS, GROUP_CHANNELS)


def prepare(place, dout, steps, rate):
    return call(
        prepare_kernel,
        [((TOKENS, 512), bf16)] * 2
        + [((HEADS, TOKENS), f32), ((TOKENS, 128), bf16), ((TOKENS, 128), bf16)],
        [], 1, place, dout, steps, rate,
    )


def forward(x, z, b, c, steps, run, run_col, state, gain, skip, after):
    def columns(array):
        return pl.BlockSpec((array.shape[0], array.shape[1] // GROUPS), lambda g: (0, g))

    def fixed(array):
        return pl.BlockSpec(array.shape, lambda g: (0, 0))

    def body(*refs):
        forward_kernel(*refs[:10], *refs[10 + len(after) :])

    wide = (TOKENS, CHANNELS)
    return pl.pallas_call(
        body,
        name="forward",
        grid=(GROUPS,),
        out_shape=[jax.ShapeDtypeStruct(wide, f32), jax.ShapeDtypeStruct(wide, bf16)],
        in_specs=[columns(x), columns(z), columns(b), columns(c), fixed(steps), fixed(run),
                  fixed(run_col), pl.BlockSpec((STATE_ROWS, N), lambda g: (g, 0)), columns(gain),
                  columns(skip)]
        + [pl.BlockSpec(memory_space=pl.ANY)] * len(after),
        out_specs=[pl.BlockSpec(WIDE, lambda g: (0, g))] * 2,
        scratch_shapes=[pltpu.VMEM((TOKENS, TOKENS), f32), pltpu.VMEM(WIDE, f32),
                        pltpu.VMEM((TOKENS, 128), f32)],
        compiler_params=pltpu.CompilerParams(vmem_limit_bytes=56 * 2**20),
        cost_estimate=pl.CostEstimate(flops=SHORT, bytes_accessed=1024, transcendentals=0),
    )(x, z, b, c, steps, run, run_col, state, gain, skip, *after)


MESSAGE = ((STATE_ROWS + 2 * PER_GROUP, N), bf16)


def norm_back(group, place, own, other, y, z, c, gain, run, run_col, first, after):
    outs = [(WIDE, bf16), (WIDE, bf16), ((1, GROUP_CHANNELS), f32), ((STATE_ROWS, N), f32), MESSAGE]
    return call(
        functools.partial(norm_back_kernel, group),
        outs + ([MESSAGE] if group else []),
        [((TOKENS, 128), f32), ((TOKENS, 128), f32)],
        1, place, own, other, (y, group), (z, group), (c, group), (gain, group), run, run_col, *first,
        flops=LONG, after=after,
    )


PART = ((QUARTER + 16, N), bf16)


def chip_state(place, keep, got):
    return call(
        chip_kernel, [PART] * 4 + [MESSAGE], [((STATE_ROWS, N), f32), ((4, 8, N), f32)],
        1, place, keep, got,
    )


def row_state(place, own, one, two, three, after):
    return call(
        row_kernel, [PART, ((4, QUARTER, N), f32), ((4, 8, N), f32)],
        [((4, QUARTER + 16, N), bf16)], 1, place, own, one, two, three, after=after,
    )


def end_state(place, one, two, three, follows, reach, after):
    return call(
        end_kernel, [((QUARTER, N), bf16)] * 4, [], 1, place, one, two, three, follows, reach,
        after=after,
    )


def last_state(place, own, one, two, three, last):
    return call(
        last_kernel, [((STATE_ROWS, N), bf16)] * 2, [((STATE_ROWS, N), bf16)],
        1, place, own, one, two, three, last,
    )


def scan_back(group, x, b, c, run, run_col, dt_col, state, grad_y, after):
    return call(
        functools.partial(scan_back_kernel, group),
        [(WIDE, f32), ((TOKENS, N), bf16), ((TOKENS, N), f32), ((2, PER_GROUP, Q), f32),
         ((TOKENS, 128), f32), ((1, 128), f32)],
        [((TOKENS, TOKENS), f32), ((TOKENS, TOKENS), f32), ((TOKENS, N), f32), ((TOKENS, 128), f32)],
        0, (x, group), (b, group), (c, group), run, run_col, dt_col, state, grad_y,
        flops=LONG, after=after,
    )


def end_back(place, *arrays, after):
    return call(
        end_back_kernel,
        [((TOKENS, CHANNELS), bf16), ((TOKENS, GROUPS * N), bf16), ((TOKENS, HEADS), f32),
         ((CHANNELS, N), f32), ((1, CHANNELS + 128), f32)],
        [((CHANNELS, N), bf16), ((HEADS, 128), f32), ((TOKENS, 128), f32), ((TOKENS, 128), f32),
         ((HEADS, 128), f32)],
        1, place, *arrays, flops=LONG, limit=32, after=after,
    )


HALF = CHANNELS // 2
TILE = 512


def weight_grad_kernel(pieces_ref, own_ref, other_ref, *refs):
    out_ref, turned = refs[-2:]

    @pl.when(pl.program_id(0) == 0)
    def _():
        for at in range(0, 2048, 512):
            turned[at : at + 512, :] = pieces_ref[at : at + 512, :].T

    right = jnp.concatenate([own_ref[...], other_ref[...]], axis=0)
    for at in range(0, 2048, 512):
        out_ref[at : at + 512, :] = dot(turned[at : at + 512, :], right).astype(bf16)


def weight_grad(pieces, own, other, after):
    return pl.pallas_call(
        weight_grad_kernel,
        name="weight_grad",
        grid=(CHANNELS // TILE,),
        out_shape=jax.ShapeDtypeStruct((2048, CHANNELS), bf16),
        in_specs=[pl.BlockSpec((2048, 512), lambda i: (0, 0))]
        + [pl.BlockSpec((TOKENS, TILE), lambda i: (0, i))] * 2
        + [pl.BlockSpec(memory_space=pl.ANY)] * len(after),
        out_specs=pl.BlockSpec((2048, TILE), lambda i: (0, i)),
        scratch_shapes=[pltpu.VMEM((2048, 512), bf16)],
        compiler_params=pltpu.CompilerParams(vmem_limit_bytes=48 * 2**20),
        cost_estimate=pl.CostEstimate(flops=SHORT, bytes_accessed=1024, transcendentals=0),
    )(pieces, own, other, *after)


NEAR = (0, -1, 1, 2)


def join_kernel(*refs):
    for half in range(2):
        for at in range(4):
            refs[8 + half][128 * at : 128 * (at + 1), :] = refs[4 * half + at][...]


def join(first, second, after):
    return call(
        join_kernel, [((512, HALF), bf16)] * 2, [], 0, *first, *second, flops=SHORT, limit=16,
        after=after,
    )


def halve_kernel(up_ref, down_ref, low_ref, high_ref):
    low_ref[...] = up_ref[:256, :]
    high_ref[...] = down_ref[256:, :]


def halve(up, down, after):
    return call(
        halve_kernel, [((256, HALF), bf16)] * 2, [], 0, up, down, flops=SHORT, limit=8, after=after
    )


def left_rows(place_ref, pieces_ref, half, firsts, second):
    left = []
    for first in firsts:
        by_y, by_z = (first, second) if half else (second, first)
        at_y, at_z = (place_ref[1] + by_y) & 3, (place_ref[2] + by_z) & 3
        rows = pl.ds(pl.multiple_of(at_y * 512, 512), 512)
        left.append(pieces_ref[rows, pl.ds(pl.multiple_of(at_z * 128, 128), 128)])
    return jnp.concatenate(left, axis=1)


def upstream_near_kernel(half, place_ref, pieces_ref, own_ref, up_ref, down_ref, *refs):
    total = None
    for second, ref in ((0, own_ref), (-1, up_ref), (1, down_ref)):
        product = dot(left_rows(place_ref, pieces_ref, half, NEAR, second), ref[...])
        total = product if total is None else total + product
    refs[-1][...] = total


def upstream_far_kernel(half, place_ref, pieces_ref, near_ref, low_ref, high_ref, *refs):
    own_ref, other_ref = refs[-2:]
    total = near_ref[...]
    total = total + dot(left_rows(place_ref, pieces_ref, half, NEAR[:2], 2), low_ref[...])
    total = total + dot(left_rows(place_ref, pieces_ref, half, NEAR[2:], 2), high_ref[...])
    own_ref[...] = total[:TOKENS]
    other_ref[...] = total[TOKENS:].astype(bf16)


def upstream(kernel, half, place, pieces, arrays, outs, after):
    return pl.pallas_call(
        functools.partial(kernel, half),
        name=f"{kernel.__name__}_{half}",
        grid=(HALF // TILE,),
        out_shape=[jax.ShapeDtypeStruct((rows, HALF), kind) for rows, kind in outs],
        in_specs=[pl.BlockSpec(memory_space=pltpu.SMEM), pl.BlockSpec((2048, 512), lambda i: (0, 0))]
        + [pl.BlockSpec((a.shape[0], TILE), lambda i: (0, i)) for a in arrays]
        + [pl.BlockSpec(memory_space=pl.ANY)] * len(after),
        out_specs=[pl.BlockSpec((rows, TILE), lambda i: (0, i)) for rows, _ in outs],
        compiler_params=pltpu.CompilerParams(vmem_limit_bytes=24 * 2**20),
        cost_estimate=pl.CostEstimate(
            flops=SHORT, bytes_accessed=1024, transcendentals=0),
    )(place, pieces, *arrays, *after)


def upstream_near(half, place, pieces, own, up, down, after):
    outs = [(2 * TOKENS, f32)]
    return upstream(upstream_near_kernel, half, place, pieces, (own, up, down), outs, after)[0]


def upstream_far(half, place, pieces, near, low, high, after):
    outs = [(TOKENS, f32), (TOKENS, bf16)]
    return upstream(upstream_far_kernel, half, place, pieces, (near, low, high), outs, after)


def device(y, z, core):
    return (y * 4 + z) * 2 + core


PLACES = [(y, z, core) for y in range(4) for z in range(4) for core in range(2)]
SAME_CORE = [[device(y, z, core) for y in range(4) for z in range(4)] for core in range(2)]
SWAP = [(device(y, z, core), device(y, z, 1 - core)) for y, z, core in PLACES]


def along_z(by):
    return [(device(y, z, core), device(y, (z + by) % 4, core)) for y, z, core in PLACES]


def along_y(by):
    return [(device(y, z, core), device((y + by) % 4, z, core)) for y, z, core in PLACES]


def earlier_y(by):
    return [(device(y, z, core), device(y - by, z, core)) for y, z, core in PLACES if y >= by]


def move(array, pairs):
    return lax.ppermute(array, "ctx", pairs)


RINGS = (
    (along_z(1), along_z(-1), along_z(2), along_y(1), along_y(-1)),
    (along_y(1), along_y(-1), along_y(2), along_z(1), along_z(-1)),
)


def sum_ctx(array):
    array = array + move(array, SWAP)
    array = array + move(array, along_z(1)) + move(array, along_z(2)) + move(array, along_z(3))
    return array + move(array, along_y(1)) + move(array, along_y(2)) + move(array, along_y(3))


def per_device(dout, out_weight, x_in, z_in, b_in, c_in, dt, rate, skip, gain, start_state):
    at = lax.axis_index("ctx")
    place = jnp.stack([lax.axis_index("head"), at // 8, (at // 2) % 4, at % 2]).astype(jnp.int32)
    steps = dt.T
    rates = rate.reshape(HEADS, 1)
    skips = jnp.repeat(skip, P_SIZE).reshape(1, CHANNELS)
    gains = gain.reshape(1, CHANNELS)
    state = start_state.reshape(CHANNELS, N)
    cut = [out_weight[:, :HALF], out_weight[:, HALF:]]
    ringed = [[cut[h]] + [move(cut[h], RINGS[h][k]) for k in range(3)] for h in range(2)]
    keep, send, run, run_col, dt_col = prepare(place, dout, steps, rates)
    both = jnp.concatenate([keep, move(send, SWAP)], axis=0)
    pieces = lax.all_gather(both, "head", axis=0, tiled=True)
    scan_in = (x_in, z_in, b_in, c_in, steps, run, run_col, state, gains, skips)
    four = join(*ringed, (run,))
    up = [move(four[h], RINGS[h][3]) for h in range(2)]
    down = [move(four[h], RINGS[h][4]) for h in range(2)]
    y, normed = forward(*scan_in, (both,))
    term = weight_grad(pieces, normed, move(normed, SWAP), ())
    grad_w = lax.psum_scatter(
        term, "ctx", scatter_dimension=0, tiled=True, axis_index_groups=SAME_CORE
    )
    ends = [halve(up[h], down[h], (term,)) for h in range(2)]
    low = [move(ends[h][0], RINGS[h][3]) for h in range(2)]
    high = [move(ends[h][1], RINGS[h][4]) for h in range(2)]
    near0 = upstream_near(0, place, pieces, four[0], up[0], down[0], (ends[1][0],))
    near1 = upstream_near(1, place, pieces, four[1], up[1], down[1], (near0,))
    part0, send0 = upstream_far(0, place, pieces, near0, low[0], high[0], (near1,))
    part1, send1 = upstream_far(1, place, pieces, near1, low[1], high[1], (part0,))
    back_in = (z_in, c_in, gains, run, run_col)
    grad_y0, grad_z0, gain_sum0, start0, message0 = norm_back(
        0, place, part0, move(send0, SWAP), y, *back_in, (), (part1,)
    )
    grad_y1, grad_z1, gain_sum1, start1, keep, send = norm_back(
        1, place, part1, move(send1, SWAP), y, *back_in, (message0,), (grad_y0,)
    )
    *quarters, last = chip_state(place, keep, move(send, SWAP))
    from_z = [move(quarters[-k], along_z(-k)) for k in (1, 2, 3)]
    back0 = scan_back(
        0, x_in, b_in, c_in, run, run_col, dt_col, state, grad_y0, (quarters[0],)
    )
    row, after, reach = row_state(place, quarters[0], *from_z, after=(back0[0],))
    from_y = [move(row, earlier_y(k)) for k in (1, 2, 3)]
    back1 = scan_back(
        1, x_in, b_in, c_in, run, run_col, dt_col, state, grad_y1, (row,)
    )
    ends = end_state(place, *from_y, after, reach, after=(back1[0],))
    mine, theirs = last_state(place, ends[0], *[move(ends[k], along_z(k)) for k in (1, 2, 3)], last)
    grad_x, grad_b, grad_dt, grad_start, sums = end_back(
        place, x_in, b_in, steps, rates, skips, run, run_col, dt_col, state, mine,
        move(theirs, SWAP),
        grad_y0, *[back0[i] for i in (0, 2, 3, 4, 5)], start0, gain_sum0,
        grad_y1, *[back1[i] for i in (0, 2, 3, 4, 5)], start1, gain_sum1,
        after=(),
    )
    sums = sum_ctx(sums)[0]
    return (
        grad_x,
        jnp.concatenate([grad_z0, grad_z1], axis=1),
        grad_b,
        jnp.concatenate([back0[1], back1[1]], axis=1),
        grad_dt,
        grad_w,
        sums[:CHANNELS],
        sums[CHANNELS + HEADS : CHANNELS + 2 * HEADS],
        sums[CHANNELS : CHANNELS + HEADS],
        grad_start.reshape(start_state.shape),
    )


def solution(mesh):
    full, whole = P("ctx", "head"), P("head")
    state = P("ctx", "head", None, None)
    return jax.shard_map(
        per_device,
        mesh=mesh,
        in_specs=(full,) * 7 + (whole,) * 3 + (state,),
        out_specs=(full,) * 6 + (whole,) * 3 + (state,),
        check_vma=False,
    )
```

```python
import functools
import math

import jax
import jax.numpy as jnp
from jax import lax
from jax.experimental import pallas as pl
from jax.experimental.pallas import tpu as pltpu
from jax.sharding import PartitionSpec as P

P_SIZE = 64
N = 128
Q = 128
TOKENS = 256
HEADS = 32
GROUPS = 2
PER_GROUP = HEADS // GROUPS
CHANNELS = HEADS * P_SIZE
GROUP_CHANNELS = PER_GROUP * P_SIZE
PAIRS = HEADS // 2
GROUP_PAIRS = PER_GROUP // 2
STATE_ROWS = PER_GROUP * P_SIZE
EPSILON = 1e-05
UNROLL = 8
SHORT, LONG = 100000000, 28000000000

f32 = jnp.float32
bf16 = jnp.bfloat16


def dot(a, b, over=((1,), (0,))):
    return lax.dot_general(a, b, (over, ((), ())), preferred_element_type=f32)


def dot_rows(a, b):
    return dot(a, b, ((1,), (1,)))


def dot_columns(a, b):
    return dot(a, b, ((0,), (0,)))


def iota(shape, axis):
    return lax.broadcasted_iota(jnp.int32, shape, axis)


def split2(v):
    high = v.astype(bf16)
    return high, (v - high.astype(f32)).astype(bf16)


def split3(v):
    high = v.astype(bf16)
    rest = v - high.astype(f32)
    middle = rest.astype(bf16)
    return high, middle, (rest - middle.astype(f32)).astype(bf16)


def exact_rows(rows, right):
    product = dot(jnp.concatenate(split3(rows), axis=0), right)
    return product[:HEADS] + product[HEADS : 2 * HEADS] + product[2 * HEADS :]


def part_columns(rows):
    parts = [part.astype(f32) for part in split3(rows)]
    stacked = jnp.concatenate(parts + [jnp.zeros_like(rows)], axis=0)
    return stacked.T.astype(bf16)


def pair_select(pair, width):
    row = iota((128, 2 * width), 0)
    head = 2 * pair + jnp.where(iota((128, 2 * width), 1) >= width, 1, 0)
    hit = ((row & (HEADS - 1)) == head) & (row < 3 * HEADS)
    return jnp.where(hit, 1.0, 0.0).astype(bf16)


def pair_sums(values, pair):
    row, lane = iota((128, 128), 0), iota((128, 128), 1)
    head = 2 * pair + jnp.where(row >= P_SIZE, 1, 0)
    place = jnp.where(lane == head, 1.0, 0.0).astype(bf16)
    high, low = split2(values)
    return dot(jnp.concatenate([high, low], axis=1), jnp.concatenate([place, place], axis=0))


def lanes_of(pair):
    return pl.ds(pl.multiple_of(pair * 128, 128), 128)


def halves(v):
    first = iota(v.shape, 1) < P_SIZE
    zero = jnp.zeros_like(v)
    return jnp.where(first, v, zero), jnp.where(first, zero, v)


def causal_exp(spread, keep):
    return jnp.exp(jnp.where(keep, spread, -1e30))


def prepare_kernel(place_ref, dout_ref, dt_ref, rate_ref, keep_ref, send_ref, run_ref, run_col_ref, dt_col_ref):
    leads = place_ref[3] == 0
    for at in range(4):
        even = dout_ref[:, 256 * at : 256 * at + 128]
        odd = dout_ref[:, 256 * at + 128 : 256 * at + 256]
        own = slice(128 * at, 128 * at + 128)
        keep_ref[:, own] = jnp.where(leads, even, odd)
        send_ref[:, own] = jnp.where(leads, odd, even)
    steps = dt_ref[...]
    upto = jnp.where(iota((TOKENS, TOKENS), 0) <= iota((TOKENS, TOKENS), 1), 1.0, 0.0).astype(bf16)
    run = exact_rows(-steps * rate_ref[...], upto)
    run_ref[...] = run
    run_col_ref[...] = part_columns(run)
    dt_col_ref[...] = part_columns(steps)


def forward_kernel(
    x_ref, z_ref, b_ref, c_ref, dt_ref, run_ref, run_col_ref, state_ref, gain_ref, skip_ref,
    y_ref, normed_ref,
    scores, gated_ref, power,
):
    group = pl.program_id(0)
    lower = iota((Q, Q), 0) >= iota((Q, Q), 1)
    reads = c_ref[...]
    scores[...] = dot_rows(reads, b_ref[...])
    power[...] = jnp.zeros_like(power)

    def body(at, carry):
        pair = group * GROUP_PAIRS + at
        lanes = own = lanes_of(at)
        xs = x_ref[:, lanes]
        expanded = dot(run_col_ref[...], pair_select(pair, 128))
        top, bottom = [], []
        for k in range(2):
            run_row = run_ref[pl.ds(2 * pair + k, 1), :]
            dt_row = dt_ref[pl.ds(2 * pair + k, 1), :]
            col = expanded[:, k * 128 : (k + 1) * 128]
            m00 = causal_exp(col[:Q] - run_row[:, :Q], lower) * (scores[:Q, :Q] * dt_row[:, :Q])
            m10 = jnp.exp(col[Q:] - run_row[:, :Q]) * (scores[Q:, :Q] * dt_row[:, :Q])
            m11 = causal_exp(col[Q:] - run_row[:, Q:], lower) * (scores[Q:, Q:] * dt_row[:, Q:])
            top.append(m00.astype(bf16))
            bottom.extend([m10.astype(bf16), m11.astype(bf16)])
        x0, x1 = halves(xs)
        y0 = dot(jnp.concatenate(top, axis=1), jnp.concatenate([x0[:Q], x1[:Q]], axis=0))
        y1 = dot(jnp.concatenate(bottom, axis=1), jnp.concatenate([x0, x1], axis=0))
        from_start = dot_rows(reads, state_ref[lanes_of(at), :].astype(bf16))
        first = iota((TOKENS, 128), 1) < P_SIZE
        reach = jnp.exp(jnp.where(first, expanded[:, :128], expanded[:, 128:]))
        y = jnp.concatenate([y0, y1], axis=0) + reach * from_start
        y = y + skip_ref[:, lanes] * xs.astype(f32)
        y_ref[:, lanes] = y
        gate = z_ref[:, lanes].astype(f32)
        gated = y * gate / (1.0 + jnp.exp(-gate))
        gated_ref[:, own] = gated
        power[...] += gated * gated
        return carry

    lax.fori_loop(0, GROUP_PAIRS, body, 0, unroll=UNROLL)
    mean = jnp.sum(power[...], axis=1, keepdims=True) * (1.0 / GROUP_CHANNELS)
    scale = jnp.broadcast_to(lax.rsqrt(mean + EPSILON), (TOKENS, 128))

    def finish(at, carry):
        lanes = own = lanes_of(at)
        normed_ref[:, lanes] = (gated_ref[:, own] * scale * gain_ref[:, lanes]).astype(bf16)
        return carry

    lax.fori_loop(0, GROUP_PAIRS, finish, 0, unroll=UNROLL)


def norm_back_kernel(
    group, place_ref, own_ref, other_ref, y_ref, z_ref, c_ref, gain_ref, run_ref, run_col_ref, *rest
):
    first_ref, rest = (rest[0], rest[1:]) if group else (None, rest)
    grad_y_ref, grad_z_ref, gain_sum_ref, start_ref = rest[:4]
    outs, (power, along) = rest[4:-2], rest[-2:]
    reads = c_ref[...]
    power[...] = jnp.zeros_like(power)
    along[...] = jnp.zeros_like(along)

    def pieces(at):
        lanes = lanes_of(at)
        upstream = own_ref[:, lanes] + other_ref[:, lanes].astype(f32)
        gate = z_ref[:, lanes].astype(f32)
        sigmoid = 1.0 / (1.0 + jnp.exp(-gate))
        y = y_ref[:, lanes]
        return lanes, upstream, gate, sigmoid, y, y * gate * sigmoid

    def first(at, carry):
        lanes, upstream, gate, sigmoid, y, gated = pieces(at)
        power[...] += gated * gated
        along[...] += upstream * gain_ref[:, lanes] * gated
        return carry

    lax.fori_loop(0, GROUP_PAIRS, first, 0, unroll=UNROLL)
    mean = jnp.sum(power[...], axis=1, keepdims=True) * (1.0 / GROUP_CHANNELS)
    scale = lax.rsqrt(mean + EPSILON)
    shared = jnp.sum(along[...], axis=1, keepdims=True) * (1.0 / GROUP_CHANNELS)
    pull = jnp.broadcast_to(scale * scale * scale * shared, (TOKENS, 128))
    scale = jnp.broadcast_to(scale, (TOKENS, 128))

    def second(at, carry):
        lanes, upstream, gate, sigmoid, y, gated = pieces(at)
        grad_gated = scale * (upstream * gain_ref[:, lanes]) - gated * pull
        grad_y = grad_gated * (gate * sigmoid)
        grad_y_ref[:, lanes] = grad_y.astype(bf16)
        slope = sigmoid * (1.0 + gate * (1.0 - sigmoid))
        grad_z_ref[:, lanes] = (grad_gated * y * slope).astype(bf16)
        gain_sum_ref[:, lanes] = jnp.sum(upstream * gated * scale, axis=0, keepdims=True)
        pair = group * GROUP_PAIRS + at
        reach = jnp.exp(dot(run_col_ref[...], pair_select(pair, P_SIZE)))
        start_ref[lanes, :] = dot_columns((grad_y * reach).astype(bf16), reads)
        return carry

    lax.fori_loop(0, GROUP_PAIRS, second, 0, unroll=UNROLL)
    total = jnp.exp(run_ref[group * PER_GROUP : (group + 1) * PER_GROUP, TOKENS - 1 :])
    high, low = split2(jnp.broadcast_to(total, (PER_GROUP, 128)))
    states = start_ref[...].astype(bf16)
    if first_ref is None:
        ref = outs[0]
        ref[:STATE_ROWS, :] = states
        ref[STATE_ROWS : STATE_ROWS + PER_GROUP, :] = high
        ref[STATE_ROWS + PER_GROUP :, :] = low
    else:
        message = jnp.concatenate([states, high, low], axis=0)
        leads = place_ref[3] == 0
        outs[0][...] = jnp.where(leads, first_ref[...], message)
        outs[1][...] = jnp.where(leads, message, first_ref[...])


QUARTER = STATE_ROWS // 4
QUARTER_HEADS = PER_GROUP // 4


def by_head(decay):
    heads = decay.shape[0]
    return jnp.broadcast_to(decay[:, None, :], (heads, P_SIZE, N)).reshape(heads * P_SIZE, N)


def decay_of(message):
    first = message[STATE_ROWS : STATE_ROWS + PER_GROUP, :].astype(f32)
    return first + message[STATE_ROWS + PER_GROUP :, :].astype(f32)


def state_of(message):
    return message[:STATE_ROWS, :].astype(f32)


def put_quarter(ref, state, decay):
    ref[:QUARTER, :] = state.astype(bf16)
    high, low = split2(decay)
    ref[QUARTER:, :] = jnp.concatenate([high.astype(f32), low.astype(f32)], axis=0).astype(bf16)


def quarter_of(message):
    decay = message[QUARTER:, :].astype(f32)
    return message[:QUARTER, :].astype(f32), decay[:8] + decay[8:]


def chip_kernel(place_ref, keep_ref, got_ref, *refs):
    outs, last_ref, states, decays = refs[:4], refs[4], refs[5], refs[6]
    leads = place_ref[3] == 0
    keep, got = keep_ref[...], got_ref[...]
    early, late = jnp.where(leads, keep, got), jnp.where(leads, got, keep)
    decay = decay_of(early)
    states[...] = state_of(early) + by_head(decay) * state_of(late)
    decay = decay * decay_of(late)
    decays[...] = jnp.zeros_like(decays)
    for at in range(4):
        decays[at, :QUARTER_HEADS, :] = decay[at * QUARTER_HEADS : (at + 1) * QUARTER_HEADS]
    for by, ref in enumerate(outs):
        at = (place_ref[2] + by) & 3
        put_quarter(ref, states[pl.ds(pl.multiple_of(at * QUARTER, QUARTER), QUARTER), :], decays[at])
    last_ref[...] = late


def row_kernel(place_ref, own_ref, one_ref, two_ref, three_ref, row_ref, after_ref, reach_ref, held):
    for k, ref in enumerate((own_ref, one_ref, two_ref, three_ref)):
        held[k] = ref[...]
    z = place_ref[2]
    state = jnp.zeros((QUARTER, N), f32)
    decay = jnp.ones((8, N), f32)
    for at in (3, 2, 1, 0):
        after_ref[at] = state
        reach_ref[at] = decay
        here_state, here = quarter_of(held[(at - z) & 3])
        state = here_state + by_head(here[:QUARTER_HEADS]) * state
        decay = here * decay
    put_quarter(row_ref, state, decay)


def end_kernel(place_ref, one_ref, two_ref, three_ref, after_ref, reach_ref, *outs):
    state = jnp.zeros((QUARTER, N), f32)
    for ref in (three_ref, two_ref, one_ref):
        here_state, here = quarter_of(ref[...])
        state = here_state + by_head(here[:QUARTER_HEADS]) * state
    for by, ref in enumerate(outs):
        at = (place_ref[2] + by) & 3
        reach = reach_ref[at]
        ref[...] = (after_ref[at] + by_head(reach[:QUARTER_HEADS]) * state).astype(bf16)


def last_kernel(place_ref, own_ref, one_ref, two_ref, three_ref, last_ref, mine_ref, send_ref, late):
    for by, ref in enumerate((own_ref, one_ref, two_ref, three_ref)):
        at = (place_ref[2] - by) & 3
        late[pl.ds(pl.multiple_of(at * QUARTER, QUARTER), QUARTER), :] = ref[...]
    message = last_ref[...]
    early = (state_of(message) + by_head(decay_of(message)) * late[...].astype(f32)).astype(bf16)
    leads = place_ref[3] == 0
    mine_ref[...] = jnp.where(leads, early, late[...])
    send_ref[...] = jnp.where(leads, late[...], early)


def scan_back_kernel(
    group, x_ref, b_ref, c_ref, run_ref, run_col_ref, dt_col_ref, state_ref, grad_y_ref,
    inner_ref, grad_c_ref, grad_b_ref, row_ref, col_ref, skip_sum_ref,
    scores, back, reads_back, skips,
):
    upper = iota((Q, Q), 0) <= iota((Q, Q), 1)
    skips[...] = jnp.zeros_like(skips)
    col_ref[...] = jnp.zeros_like(col_ref)
    lane = iota((Q, 128), 1)
    keys = b_ref[...]
    reads = c_ref[...]
    scores[...] = dot_rows(keys, reads)
    back[...] = jnp.zeros_like(back)
    reads_back[...] = jnp.zeros_like(reads_back)

    def body(at, carry):
        pair = group * GROUP_PAIRS + at
        lanes = lanes_of(at)
        xs = x_ref[:, lanes].astype(f32)
        grads = grad_y_ref[:, lanes]
        step = dot(dt_col_ref[...], pair_select(pair, P_SIZE))
        scaled = halves((step * xs).astype(bf16))
        split = halves(grads)
        expanded = dot(run_col_ref[...], pair_select(pair, 128))
        top, bottom = [], []
        for k in range(2):
            head = 2 * pair + k
            run_row = run_ref[pl.ds(head, 1), :]
            col = expanded[:, k * 128 : (k + 1) * 128]
            d0 = dot_rows(scaled[k][:Q], grads)
            d11 = dot_rows(scaled[k][Q:], grads[Q:])
            l00 = causal_exp(run_row[:, :Q] - col[:Q], upper)
            l01 = jnp.exp(run_row[:, Q:] - col[:Q])
            l11 = causal_exp(run_row[:, Q:] - col[Q:], upper)
            p00, p01, p11 = l00 * d0[:, :Q], l01 * d0[:, Q:], l11 * d11
            back[:Q, :Q] += p00
            back[:Q, Q:] += p01
            back[Q:, Q:] += p11
            s00, s01, s11 = scores[:Q, :Q], scores[:Q, Q:], scores[Q:, Q:]
            w00, w01, w11 = p00 * s00, p01 * s01, p11 * s11
            row_ref[0, pl.ds(2 * at + k, 1), :] = jnp.sum(w00, axis=0, keepdims=True)
            row_ref[1, pl.ds(2 * at + k, 1), :] = jnp.sum(w01 + w11, axis=0, keepdims=True)
            col_ref[:Q, :] -= jnp.where(lane == head, jnp.sum(w00 + w01, axis=1, keepdims=True), 0.0)
            col_ref[Q:, :] -= jnp.where(lane == head, jnp.sum(w11, axis=1, keepdims=True), 0.0)
            top.extend([(l00 * s00).astype(bf16), (l01 * s01).astype(bf16)])
            bottom.append((l11 * s11).astype(bf16))
        inner_ref[:Q, lanes] = dot(jnp.concatenate(top, axis=1), jnp.concatenate(split, axis=0))
        inner_ref[Q:, lanes] = dot(
            jnp.concatenate(bottom, axis=1),
            jnp.concatenate([split[0][Q:], split[1][Q:]], axis=0),
        )
        state = state_ref[lanes_of(pair), :].astype(bf16)
        first = iota((TOKENS, 128), 1) < P_SIZE
        reach = jnp.exp(jnp.where(first, expanded[:, :128], expanded[:, 128:]))
        wide = grads.astype(f32)
        reached = reach * wide
        reads_back[...] += dot(reached.astype(bf16), state)
        col_ref[...] += pair_sums(reached * dot_rows(reads, state), pair)
        skips[...] += pair_sums(xs * wide, pair)
        return carry

    lax.fori_loop(0, GROUP_PAIRS, body, 0, unroll=UNROLL)
    inner = back[...].astype(bf16)
    grad_b_ref[...] = dot(inner, reads)
    grad_c_ref[...] = (
        dot_columns(inner, keys) + reads_back[...]
    ).astype(bf16)
    skip_sum_ref[...] = jnp.sum(skips[...], axis=0, keepdims=True)


def end_back_kernel(
    place_ref, x_ref, b_ref, dt_ref, rate_ref, skip_ref, run_ref, run_col_ref, dt_col_ref,
    state_ref, mine_ref, got_ref, *refs
):
    per_group, rest = (refs[:8], refs[8:16]), refs[16:]
    end_back_body(
        place_ref, x_ref, b_ref, dt_ref, rate_ref, skip_ref, run_ref, run_col_ref, dt_col_ref,
        state_ref, mine_ref, got_ref, per_group, *rest
    )


def end_back_body(
    place_ref, x_ref, b_ref, dt_ref, rate_ref, skip_ref, run_ref, run_col_ref, dt_col_ref,
    state_ref, mine_ref, got_ref, per_group,
    grad_x_ref, grad_b_ref, grad_dt_ref, grad_start_ref, sums_ref,
    ends, decay, directs, tails, products,
):
    core = place_ref[3]
    ends[pl.ds(pl.multiple_of(core * STATE_ROWS, STATE_ROWS), STATE_ROWS), :] = mine_ref[...]
    ends[pl.ds(pl.multiple_of((1 - core) * STATE_ROWS, STATE_ROWS), STATE_ROWS), :] = got_ref[...]
    run = run_ref[...]
    total = jnp.exp(run[:, TOKENS - 1 : TOKENS])
    decay[...] = jnp.broadcast_to(total, (HEADS, 128))
    directs[...] = jnp.zeros_like(directs)
    tails[...] = jnp.zeros_like(tails)
    for group in range(GROUPS):
        grad_y_ref, inner_ref, keys_back_ref, _, _, _, start_ref, _ = per_group[group]
        keys = b_ref[:, group * N : (group + 1) * N]

        def body(at, keys_back):
            pair = group * GROUP_PAIRS + at
            lanes, local = lanes_of(pair), lanes_of(at)
            end = ends[lanes, :]
            wide_end = end.astype(f32)
            xs = x_ref[:, lanes].astype(f32)
            step = dot(dt_col_ref[...], pair_select(pair, P_SIZE))
            running = dot(run_col_ref[...], pair_select(pair, P_SIZE))
            tail = jnp.exp(running[TOKENS - 1 :, :] - running)
            read = dot_rows(keys, end)
            tailed = tail * (step * xs)
            grad_scaled = inner_ref[:, local] + tail * read
            grad_x = step * grad_scaled + skip_ref[:, lanes] * grad_y_ref[:, local].astype(f32)
            grad_x_ref[:, lanes] = grad_x.astype(bf16)
            directs[...] += pair_sums(xs * grad_scaled, pair)
            tails[...] += pair_sums(tailed * read, pair)
            product = wide_end * state_ref[lanes, :]
            for k in range(2):
                head = 2 * pair + k
                half = slice(k * P_SIZE, (k + 1) * P_SIZE)
                products[pl.ds(head, 1), :] = jnp.sum(product[half], axis=0, keepdims=True)
                rows = pl.ds(pl.multiple_of(head * P_SIZE, P_SIZE), P_SIZE)
                own = pl.ds(pl.multiple_of((2 * at + k) * P_SIZE, P_SIZE), P_SIZE)
                grad_start_ref[rows, :] = start_ref[own, :] + decay[pl.ds(head, 1), :] * wide_end[half]
            return keys_back + dot(tailed.astype(bf16), end)

        keys_back = lax.fori_loop(
            0, GROUP_PAIRS, body, keys_back_ref[...], unroll=UNROLL
        )
        grad_b_ref[:, group * N : (group + 1) * N] = keys_back.astype(bf16)
    tail_rows = tails[...].T[:HEADS]
    shared = jnp.sum(tail_rows, axis=1, keepdims=True)
    shared = shared + total * jnp.sum(products[...], axis=1, keepdims=True)
    rows = [jnp.concatenate([group[3][0], group[3][1]], axis=1) for group in per_group]
    columns = per_group[0][4][...] + per_group[1][4][...] - tails[...]
    here = jnp.concatenate(rows, axis=0) + columns.T[:HEADS]
    since = jnp.where(iota((TOKENS, TOKENS), 0) >= iota((TOKENS, TOKENS), 1), 1.0, 0.0).astype(bf16)
    grad_log = exact_rows(here, since) + shared
    grad_dt = directs[...].T[:HEADS] - rate_ref[...] * grad_log
    spent = -dt_ref[...] * grad_log
    zero = jnp.zeros_like(spent)
    columns = jnp.concatenate([grad_dt, spent, zero, zero], axis=0).T
    grad_dt_ref[...] = columns[:, :HEADS]
    sums = jnp.sum(columns, axis=0, keepdims=True)
    for group in range(GROUPS):
        own = slice(group * GROUP_CHANNELS, (group + 1) * GROUP_CHANNELS)
        sums_ref[:, own] = per_group[group][7][...]
    skips = per_group[0][5][...] + per_group[1][5][...]
    sums_ref[:, CHANNELS:] = jnp.where(iota((1, 128), 1) < HEADS, skips, sums)


def call(kernel, outs, scratch, scalars, *arrays, flops=0, limit=24, after=()):
    specs = [pl.BlockSpec(memory_space=pltpu.SMEM)] * scalars
    plain, size = list(arrays[:scalars]), 0
    for array in arrays[scalars:]:
        array, group = array if isinstance(array, tuple) else (array, None)
        shape = array.shape
        if group is None:
            specs.append(pl.BlockSpec(shape, lambda i, n=len(shape): (0,) * n))
        else:
            shape = shape[:-1] + (shape[-1] // GROUPS,)
            specs.append(pl.BlockSpec(shape, lambda i, group=group: (0, group)))
        size += math.prod(shape) * array.dtype.itemsize
        plain.append(array)
    size += sum(math.prod(shape) * jnp.dtype(kind).itemsize for shape, kind in outs)
    used = len(plain)

    def body(*refs):
        kernel(*refs[:used], *refs[used + len(after) :])

    return pl.pallas_call(
        body,
        grid=(1,),
        out_shape=[jax.ShapeDtypeStruct(shape, kind) for shape, kind in outs],
        in_specs=specs + [pl.BlockSpec(memory_space=pl.ANY)] * len(after),
        out_specs=[pl.BlockSpec(shape, lambda i, n=len(shape): (0,) * n) for shape, _ in outs],
        scratch_shapes=[pltpu.VMEM(shape, kind) for shape, kind in scratch],
        name=getattr(kernel, "func", kernel).__name__,
        compiler_params=pltpu.CompilerParams(vmem_limit_bytes=limit * 2**20),
        cost_estimate=pl.CostEstimate(flops=flops, bytes_accessed=size, transcendentals=0),
    )(*plain, *after)


WIDE = (TOKENS, GROUP_CHANNELS)


def prepare(place, dout, steps, rate):
    return call(
        prepare_kernel,
        [((TOKENS, 512), bf16)] * 2
        + [((HEADS, TOKENS), f32), ((TOKENS, 128), bf16), ((TOKENS, 128), bf16)],
        [], 1, place, dout, steps, rate,
    )


def forward(x, z, b, c, steps, run, run_col, state, gain, skip, after):
    def columns(array):
        return pl.BlockSpec((array.shape[0], array.shape[1] // GROUPS), lambda g: (0, g))

    def fixed(array):
        return pl.BlockSpec(array.shape, lambda g: (0, 0))

    def body(*refs):
        forward_kernel(*refs[:10], *refs[10 + len(after) :])

    wide = (TOKENS, CHANNELS)
    return pl.pallas_call(
        body,
        name="forward",
        grid=(GROUPS,),
        out_shape=[jax.ShapeDtypeStruct(wide, f32), jax.ShapeDtypeStruct(wide, bf16)],
        in_specs=[columns(x), columns(z), columns(b), columns(c), fixed(steps), fixed(run),
                  fixed(run_col), pl.BlockSpec((STATE_ROWS, N), lambda g: (g, 0)), columns(gain),
                  columns(skip)]
        + [pl.BlockSpec(memory_space=pl.ANY)] * len(after),
        out_specs=[pl.BlockSpec(WIDE, lambda g: (0, g))] * 2,
        scratch_shapes=[pltpu.VMEM((TOKENS, TOKENS), f32), pltpu.VMEM(WIDE, f32),
                        pltpu.VMEM((TOKENS, 128), f32)],
        compiler_params=pltpu.CompilerParams(vmem_limit_bytes=56 * 2**20),
        cost_estimate=pl.CostEstimate(flops=SHORT, bytes_accessed=1024, transcendentals=0),
    )(x, z, b, c, steps, run, run_col, state, gain, skip, *after)


MESSAGE = ((STATE_ROWS + 2 * PER_GROUP, N), bf16)


def norm_back(group, place, own, other, y, z, c, gain, run, run_col, first, after):
    outs = [(WIDE, bf16), (WIDE, bf16), ((1, GROUP_CHANNELS), f32), ((STATE_ROWS, N), f32), MESSAGE]
    return call(
        functools.partial(norm_back_kernel, group),
        outs + ([MESSAGE] if group else []),
        [((TOKENS, 128), f32), ((TOKENS, 128), f32)],
        1, place, own, other, (y, group), (z, group), (c, group), (gain, group), run, run_col, *first,
        flops=LONG, after=after,
    )


PART = ((QUARTER + 16, N), bf16)


def chip_state(place, keep, got):
    return call(
        chip_kernel, [PART] * 4 + [MESSAGE], [((STATE_ROWS, N), f32), ((4, 8, N), f32)],
        1, place, keep, got,
    )


def row_state(place, own, one, two, three, after):
    return call(
        row_kernel, [PART, ((4, QUARTER, N), f32), ((4, 8, N), f32)],
        [((4, QUARTER + 16, N), bf16)], 1, place, own, one, two, three, after=after,
    )


def end_state(place, one, two, three, follows, reach, after):
    return call(
        end_kernel, [((QUARTER, N), bf16)] * 4, [], 1, place, one, two, three, follows, reach,
        after=after,
    )


def last_state(place, own, one, two, three, last):
    return call(
        last_kernel, [((STATE_ROWS, N), bf16)] * 2, [((STATE_ROWS, N), bf16)],
        1, place, own, one, two, three, last,
    )


def scan_back(group, x, b, c, run, run_col, dt_col, state, grad_y, after):
    return call(
        functools.partial(scan_back_kernel, group),
        [(WIDE, f32), ((TOKENS, N), bf16), ((TOKENS, N), f32), ((2, PER_GROUP, Q), f32),
         ((TOKENS, 128), f32), ((1, 128), f32)],
        [((TOKENS, TOKENS), f32), ((TOKENS, TOKENS), f32), ((TOKENS, N), f32), ((TOKENS, 128), f32)],
        0, (x, group), (b, group), (c, group), run, run_col, dt_col, state, grad_y,
        flops=LONG, after=after,
    )


def end_back(place, *arrays, after):
    return call(
        end_back_kernel,
        [((TOKENS, CHANNELS), bf16), ((TOKENS, GROUPS * N), bf16), ((TOKENS, HEADS), f32),
         ((CHANNELS, N), f32), ((1, CHANNELS + 128), f32)],
        [((CHANNELS, N), bf16), ((HEADS, 128), f32), ((TOKENS, 128), f32), ((TOKENS, 128), f32),
         ((HEADS, 128), f32)],
        1, place, *arrays, flops=LONG, limit=32, after=after,
    )


HALF = CHANNELS // 2
TILE = 512


def weight_grad_kernel(pieces_ref, own_ref, other_ref, *refs):
    out_ref, turned = refs[-2:]

    @pl.when(pl.program_id(0) == 0)
    def _():
        for at in range(0, 2048, 512):
            turned[at : at + 512, :] = pieces_ref[at : at + 512, :].T

    right = jnp.concatenate([own_ref[...], other_ref[...]], axis=0)
    for at in range(0, 2048, 512):
        out_ref[at : at + 512, :] = dot(turned[at : at + 512, :], right).astype(bf16)


def weight_grad(pieces, own, other, after):
    return pl.pallas_call(
        weight_grad_kernel,
        name="weight_grad",
        grid=(CHANNELS // TILE,),
        out_shape=jax.ShapeDtypeStruct((2048, CHANNELS), bf16),
        in_specs=[pl.BlockSpec((2048, 512), lambda i: (0, 0))]
        + [pl.BlockSpec((TOKENS, TILE), lambda i: (0, i))] * 2
        + [pl.BlockSpec(memory_space=pl.ANY)] * len(after),
        out_specs=pl.BlockSpec((2048, TILE), lambda i: (0, i)),
        scratch_shapes=[pltpu.VMEM((2048, 512), bf16)],
        compiler_params=pltpu.CompilerParams(vmem_limit_bytes=48 * 2**20),
        cost_estimate=pl.CostEstimate(flops=SHORT, bytes_accessed=1024, transcendentals=0),
    )(pieces, own, other, *after)


NEAR = (0, -1, 1, 2)


def join_kernel(*refs):
    for half in range(2):
        for at in range(4):
            refs[8 + half][128 * at : 128 * (at + 1), :] = refs[4 * half + at][...]


def join(first, second, after):
    return call(
        join_kernel, [((512, HALF), bf16)] * 2, [], 0, *first, *second, flops=SHORT, limit=16,
        after=after,
    )


def halve_kernel(up_ref, down_ref, low_ref, high_ref):
    low_ref[...] = up_ref[:256, :]
    high_ref[...] = down_ref[256:, :]


def halve(up, down, after):
    return call(
        halve_kernel, [((256, HALF), bf16)] * 2, [], 0, up, down, flops=SHORT, limit=8, after=after
    )


def left_rows(place_ref, pieces_ref, half, firsts, second):
    left = []
    for first in firsts:
        by_y, by_z = (first, second) if half else (second, first)
        at_y, at_z = (place_ref[1] + by_y) & 3, (place_ref[2] + by_z) & 3
        rows = pl.ds(pl.multiple_of(at_y * 512, 512), 512)
        left.append(pieces_ref[rows, pl.ds(pl.multiple_of(at_z * 128, 128), 128)])
    return jnp.concatenate(left, axis=1)


def upstream_near_kernel(half, place_ref, pieces_ref, own_ref, up_ref, down_ref, *refs):
    total = None
    for second, ref in ((0, own_ref), (-1, up_ref), (1, down_ref)):
        product = dot(left_rows(place_ref, pieces_ref, half, NEAR, second), ref[...])
        total = product if total is None else total + product
    refs[-1][...] = total


def upstream_far_kernel(half, place_ref, pieces_ref, near_ref, low_ref, high_ref, *refs):
    own_ref, other_ref = refs[-2:]
    total = near_ref[...]
    total = total + dot(left_rows(place_ref, pieces_ref, half, NEAR[:2], 2), low_ref[...])
    total = total + dot(left_rows(place_ref, pieces_ref, half, NEAR[2:], 2), high_ref[...])
    own_ref[...] = total[:TOKENS]
    other_ref[...] = total[TOKENS:].astype(bf16)


def upstream(kernel, half, place, pieces, arrays, outs, after):
    return pl.pallas_call(
        functools.partial(kernel, half),
        name=f"{kernel.__name__}_{half}",
        grid=(HALF // TILE,),
        out_shape=[jax.ShapeDtypeStruct((rows, HALF), kind) for rows, kind in outs],
        in_specs=[pl.BlockSpec(memory_space=pltpu.SMEM), pl.BlockSpec((2048, 512), lambda i: (0, 0))]
        + [pl.BlockSpec((a.shape[0], TILE), lambda i: (0, i)) for a in arrays]
        + [pl.BlockSpec(memory_space=pl.ANY)] * len(after),
        out_specs=[pl.BlockSpec((rows, TILE), lambda i: (0, i)) for rows, _ in outs],
        compiler_params=pltpu.CompilerParams(vmem_limit_bytes=24 * 2**20),
        cost_estimate=pl.CostEstimate(
            flops=SHORT, bytes_accessed=1024, transcendentals=0),
    )(place, pieces, *arrays, *after)


def upstream_near(half, place, pieces, own, up, down, after):
    outs = [(2 * TOKENS, f32)]
    return upstream(upstream_near_kernel, half, place, pieces, (own, up, down), outs, after)[0]


def upstream_far(half, place, pieces, near, low, high, after):
    outs = [(TOKENS, f32), (TOKENS, bf16)]
    return upstream(upstream_far_kernel, half, place, pieces, (near, low, high), outs, after)


def device(y, z, core):
    return (y * 4 + z) * 2 + core


PLACES = [(y, z, core) for y in range(4) for z in range(4) for core in range(2)]
SAME_CORE = [[device(y, z, core) for y in range(4) for z in range(4)] for core in range(2)]
SWAP = [(device(y, z, core), device(y, z, 1 - core)) for y, z, core in PLACES]


def along_z(by):
    return [(device(y, z, core), device(y, (z + by) % 4, core)) for y, z, core in PLACES]


def along_y(by):
    return [(device(y, z, core), device((y + by) % 4, z, core)) for y, z, core in PLACES]


def earlier_y(by):
    return [(device(y, z, core), device(y - by, z, core)) for y, z, core in PLACES if y >= by]


def move(array, pairs):
    return lax.ppermute(array, "ctx", pairs)


RINGS = (
    (along_z(1), along_z(-1), along_z(2), along_y(1), along_y(-1)),
    (along_y(1), along_y(-1), along_y(2), along_z(1), along_z(-1)),
)


def sum_ctx(array):
    array = array + move(array, SWAP)
    array = array + move(array, along_z(1)) + move(array, along_z(2)) + move(array, along_z(3))
    return array + move(array, along_y(1)) + move(array, along_y(2)) + move(array, along_y(3))


def per_device(dout, out_weight, x_in, z_in, b_in, c_in, dt, rate, skip, gain, start_state):
    at = lax.axis_index("ctx")
    place = jnp.stack([lax.axis_index("head"), at // 8, (at // 2) % 4, at % 2]).astype(jnp.int32)
    steps = dt.T
    rates = rate.reshape(HEADS, 1)
    skips = jnp.repeat(skip, P_SIZE).reshape(1, CHANNELS)
    gains = gain.reshape(1, CHANNELS)
    state = start_state.reshape(CHANNELS, N)
    cut = [out_weight[:, :HALF], out_weight[:, HALF:]]
    ringed = [[cut[h]] + [move(cut[h], RINGS[h][k]) for k in range(3)] for h in range(2)]
    keep, send, run, run_col, dt_col = prepare(place, dout, steps, rates)
    both = jnp.concatenate([keep, move(send, SWAP)], axis=0)
    pieces = lax.all_gather(both, "head", axis=0, tiled=True)
    scan_in = (x_in, z_in, b_in, c_in, steps, run, run_col, state, gains, skips)
    four = join(*ringed, (run,))
    up = [move(four[h], RINGS[h][3]) for h in range(2)]
    down = [move(four[h], RINGS[h][4]) for h in range(2)]
    y, normed = forward(*scan_in, (both,))
    term = weight_grad(pieces, normed, move(normed, SWAP), ())
    grad_w = lax.psum_scatter(
        term, "ctx", scatter_dimension=0, tiled=True, axis_index_groups=SAME_CORE
    )
    ends = [halve(up[h], down[h], (term,)) for h in range(2)]
    low = [move(ends[h][0], RINGS[h][3]) for h in range(2)]
    high = [move(ends[h][1], RINGS[h][4]) for h in range(2)]
    near0 = upstream_near(0, place, pieces, four[0], up[0], down[0], (ends[1][0],))
    near1 = upstream_near(1, place, pieces, four[1], up[1], down[1], (near0,))
    part0, send0 = upstream_far(0, place, pieces, near0, low[0], high[0], (near1,))
    part1, send1 = upstream_far(1, place, pieces, near1, low[1], high[1], (part0,))
    back_in = (z_in, c_in, gains, run, run_col)
    grad_y0, grad_z0, gain_sum0, start0, message0 = norm_back(
        0, place, part0, move(send0, SWAP), y, *back_in, (), (part1,)
    )
    grad_y1, grad_z1, gain_sum1, start1, keep, send = norm_back(
        1, place, part1, move(send1, SWAP), y, *back_in, (message0,), (grad_y0,)
    )
    *quarters, last = chip_state(place, keep, move(send, SWAP))
    from_z = [move(quarters[-k], along_z(-k)) for k in (1, 2, 3)]
    back0 = scan_back(
        0, x_in, b_in, c_in, run, run_col, dt_col, state, grad_y0, (quarters[0],)
    )
    row, after, reach = row_state(place, quarters[0], *from_z, after=(back0[0],))
    from_y = [move(row, earlier_y(k)) for k in (1, 2, 3)]
    back1 = scan_back(
        1, x_in, b_in, c_in, run, run_col, dt_col, state, grad_y1, (row,)
    )
    ends = end_state(place, *from_y, after, reach, after=(back1[0],))
    mine, theirs = last_state(place, ends[0], *[move(ends[k], along_z(k)) for k in (1, 2, 3)], last)
    grad_x, grad_b, grad_dt, grad_start, sums = end_back(
        place, x_in, b_in, steps, rates, skips, run, run_col, dt_col, state, mine,
        move(theirs, SWAP),
        grad_y0, *[back0[i] for i in (0, 2, 3, 4, 5)], start0, gain_sum0,
        grad_y1, *[back1[i] for i in (0, 2, 3, 4, 5)], start1, gain_sum1,
        after=(),
    )
    sums = sum_ctx(sums)[0]
    return (
        grad_x,
        jnp.concatenate([grad_z0, grad_z1], axis=1),
        grad_b,
        jnp.concatenate([back0[1], back1[1]], axis=1),
        grad_dt,
        grad_w,
        sums[:CHANNELS],
        sums[CHANNELS + HEADS : CHANNELS + 2 * HEADS],
        sums[CHANNELS : CHANNELS + HEADS],
        grad_start.reshape(start_state.shape),
    )


def solution(mesh):
    full, whole = P("ctx", "head"), P("head")
    state = P("ctx", "head", None, None)
    return jax.shard_map(
        per_device,
        mesh=mesh,
        in_specs=(full,) * 7 + (whole,) * 3 + (state,),
        out_specs=(full,) * 6 + (whole,) * 3 + (state,),
        check_vma=False,
    )
```
